128 devices in a mesh: grp: 4 (over x), smp: 32 (over y, z, core).
Axes of the slice: x: 4, y: 4, z: 4, core: 2. Of those that a mesh axis runs over, the one named last changes fastest.
Arguments:
- hidden: bfloat16 [4, 128, 4, 3584], P('grp', 'smp'), may hold values from -3 to 3
- query: bfloat16 [4, 128, 4, 64, 576], P('grp', 'smp'), may hold values from -40 to 40
- prefill_cache: bfloat16 [4, 8, 2048, 576], P('grp', None, 'smp'), may hold values from -4.5 to 4.5
- suffix_cache: bfloat16 [4, 128, 128, 576], P('grp', 'smp'), may hold values from -4 to 4
- suffix_len: int32 [4, 128], P('grp', 'smp'), may hold values from 1 to 128, 8192 in all within a row
- new_latent: bfloat16 [4, 128, 4, 576], P('grp', 'smp'), may hold values from -4 to 4
- w_uv: bfloat16 [64, 512, 128], P('smp'), may hold values from -0.25 to 0.25
- w_out: bfloat16 [64, 128, 3584], P('smp'), may hold values from -0.25 to 0.25
- ffn_gain: bfloat16 [3584], replicated, may hold values from 0.099609375 to 1.8984375
- expert_ids: int32 [4, 128, 4, 8], P('grp', 'smp'), may hold values from 0 to 127, all different within a row; in each aligned block of 16 rows (0 to 15, 16 to 31, ..., all dimensions but the last counted through in order) at most 2 rows name the same one
- route_weights: float32 [4, 128, 4, 8], P('grp', 'smp'), may hold values from 0.05 to 0.5
- w_gate: bfloat16 [128, 3584, 1024], P(('grp', 'smp')), may hold values from -0.09375 to 0.09375
- w_up: bfloat16 [128, 3584, 1024], P(('grp', 'smp')), may hold values from -0.09375 to 0.09375
- w_down: bfloat16 [128, 1024, 3584], P(('grp', 'smp')), may hold values from -0.1875 to 0.1875
Outputs:
- layer_out: bfloat16 [4, 128, 4, 3584], P('grp', 'smp')
The draws below stay inside these ranges and needn't reach their ends.
Inputs may be any that keep to these rules, and one draw needn't show every extreme that they name: `expert_ids`: the rows of one device name one expert at most 2 times; every expert is named by some row.
All inputs are finite; a program needn't handle non-finite values. No bound on the sum of `suffix_len` on one device may be relied on, other than what follows from the above.
Results may differ from the reference program's by a relative error of at most 0.024.
Values may be sent and summed in bfloat16 or wider, within the bound.
No kernel may reach another device: no remote copies, remote signals or barrier semaphores. Data moves between devices by JAX's collectives and lax.ppermute only.
A program may use at most 128 MiB of HBM per device.

```python
import math
import jax
import jax.numpy as jnp
import numpy as np
from jax import lax

D = 3584
HEADS = 64
LAT = 512
ROPE = 64
NOPE = 128
FF = 1024
TOP = 8
EXPERTS = 128
GROUP = 16
STEPS = 4
SUF = 128
TOK_DEV = 16
ROLLOUTS = 128
PROMPTS = 8
PREFIX = 2048
CAP = 2
N_GRP = 4
N_SMP = 32


def latent_pool(key):
    key_width = LAT + ROPE
    prefix_keys = jax.random.truncated_normal(jax.random.fold_in(key, 102), -4.0, 4.0, (N_GRP, PROMPTS, PREFIX, key_width), jnp.float32)
    twin_row = prefix_keys[:, :, PREFIX - 2]
    prefix_keys = prefix_keys.at[:, :, PREFIX - 2].set(twin_row)
    own_keys = jax.random.truncated_normal(jax.random.fold_in(key, 104), -4.0, 4.0, (N_GRP, ROLLOUTS, SUF, key_width), jnp.float32)
    fresh_keys = jax.random.truncated_normal(jax.random.fold_in(key, 105), -4.0, 4.0, (N_GRP, ROLLOUTS, STEPS, key_width), jnp.float32)
    return (prefix_keys, own_keys, fresh_keys)


def draw_prefill_cache(key, part):
    pooled = latent_pool(key)
    return pooled[0].astype(jnp.bfloat16)


def draw_suffix_cache(key, part):
    pooled = latent_pool(key)
    return pooled[1].astype(jnp.bfloat16)


def draw_new_latent(key, part):
    pooled = latent_pool(key)
    return pooled[2].astype(jnp.bfloat16)


def draw_query(key, part):
    prefix_keys, own_keys, fresh_keys = latent_pool(key)
    key = jax.random.fold_in(key, 7)
    key_width = LAT + ROPE
    base = jax.random.truncated_normal(key, -4.0, 4.0, (N_GRP, ROLLOUTS, STEPS, HEADS, key_width), jnp.float32)
    queries = base + 0.15 * fresh_keys[:, :, :, None, :]
    return queries.astype(jnp.bfloat16)


def shard_levels(stream_key, dims, shards, smallest, largest):
    gain, own = 1.0, jax.random.fold_in(stream_key, 6)
    for dim, blocks in shards:
        steps = jnp.exp(jax.random.uniform(jax.random.fold_in(own, dim), (blocks,), jnp.float32, smallest / len(shards), largest / len(shards)))
        gain = gain * jnp.repeat(steps, dims[dim] // blocks).reshape([-1 if axis == dim else 1 for axis in range(len(dims))])
    return gain


def split_up(count, total, reach, slope):
    loads = [(1 << 20) // math.isqrt(grade ** slope) + 1 for grade in range(2, count + 1)]
    surplus, holding = total - reach - (count - 1), [1] * (count - 1)
    while surplus > 0:
        candidates = [i for i in range(count - 1) if holding[i] < reach]
        pool, left = sum([loads[i] for i in candidates]), surplus
        for i in candidates:
            addition = min(reach - holding[i], max(1, left * loads[i] // pool), surplus)
            holding[i] = holding[i] + addition
            surplus = surplus - addition
    return np.array([reach] + holding)


def ragged_sizes(rng, count, total, limit, slope):
    if count == 2:
        one = jax.random.randint(rng, (), max(1, total - limit), min(limit, total - 1) + 1)
        return jnp.stack([one, total - one])
    lengths = jnp.asarray(split_up(count, total, limit, slope), jnp.int32)
    couples = (count - 1) // 2
    donor, sink = lengths[1:1 + 2 * couples:2], lengths[2:2 + 2 * couples:2]
    room = jnp.minimum(donor - 1, limit - sink)
    shifted = jax.random.randint(jax.random.fold_in(rng, 1), (couples,), 0, 1 << 20) % (room + 1)
    lengths = lengths.at[1:1 + 2 * couples:2].set(donor - shifted).at[2:2 + 2 * couples:2].set(sink + shifted)
    return lengths[jax.random.permutation(jax.random.fold_in(rng, 2), count)]


def shared_out(own_key, own, number, rows, count, top, limit, slope):
    sequence = jax.random.permutation(own_key, count)
    crowded, ordinary = shares(count, rows * top, limit, slope, True), shares(count, rows * top, limit, slope, False)
    places = jnp.arange(count)

    def named(sizes, rotation):
        used = int((sizes > 0).sum())
        fixed = max(1, used // 4)
        passed = fixed + (places - fixed + rotation * (used - fixed)) % max(1, count - fixed)
        return jnp.zeros((count,), jnp.int32).at[sequence[jnp.where(places < fixed, places, passed)]].set(jnp.asarray(sizes, jnp.int32))

    sizes = jnp.where(number % 4 == 0, named(crowded, number // 4), named(ordinary, number - number // 4 - 1))
    mixed = jax.random.permutation(jax.random.fold_in(own, 3), count)
    donor, receiver = mixed[0:count // 2 * 2:2], mixed[1:count // 2 * 2:2]
    room = jnp.minimum(sizes[donor] - 1, limit - sizes[receiver]) // 2
    room = jnp.where((donor == sequence[0]) | (receiver == sequence[0]) | (sizes[receiver] == 0), 0, jnp.maximum(room, 0))
    passed = jax.random.randint(jax.random.fold_in(own, 4), (count // 2,), 0, 1 << 20) % (room + 1)
    sizes = sizes.at[donor].add(-passed).at[receiver].add(passed)
    items = jnp.searchsorted(jnp.cumsum(sizes), jnp.arange(rows * top), side="right").astype(jnp.int32)
    table = items.reshape(top, rows).T
    table = table[jax.random.permutation(jax.random.fold_in(own, 1), rows)]
    rotation = jax.random.randint(jax.random.fold_in(own, 2), (rows, 1), 0, top)
    return jnp.take_along_axis(table, (jnp.arange(top)[None, :] + rotation) % top, axis=1)


def shares(number_of, total, limit, skew, full):
    weights = [(1 << 20) // math.isqrt(standing ** skew) + 1 for standing in range(1, number_of + 1)]
    largest = limit if full else min(limit, max(-(-total // number_of), total * weights[0] // sum(weights)))
    least = 1 if total - largest >= number_of - 1 else 0
    given, spare = [largest] + [least] * (number_of - 1), total - largest - least * (number_of - 1)
    while spare > 0:
        free = [i for i in range(1, number_of) if given[i] < largest] or [i for i in range(1, number_of) if given[i] < limit]
        pool, remaining = sum([weights[i] for i in free]), spare
        for i in free:
            addition = min(limit - given[i], max(1, remaining * weights[i] // pool), spare)
            given[i] = given[i] + addition
            spare = spare - addition
    return np.array(given)


def scatter_about(own_key, shape, width, bound, split=(), kind=jnp.bfloat16):
    factor_of = shard_levels(own_key, shape, split, -0.22, 0.18) if split else 1.0
    entries = jax.random.normal(own_key, shape, jnp.float32) * width * factor_of
    return jnp.minimum(jnp.maximum(entries, -bound), bound).astype(kind)


def setup_inputs(seed: int = 0) -> dict:
    keys = jax.random.split(jax.random.key(seed), 15)
    hidden = scatter_about(keys[0], (N_GRP, ROLLOUTS, STEPS, D), 0.5, 3.0, ((0, 4), (1, 32)))
    query = draw_query(jax.random.fold_in(keys[14], 71), 0)
    prefill_cache = draw_prefill_cache(jax.random.fold_in(keys[14], 71), 0)
    suffix_cache = draw_suffix_cache(jax.random.fold_in(keys[14], 71), 0)
    suffix_len = jax.vmap(lambda own: ragged_sizes(own, ROLLOUTS, ROLLOUTS * SUF // 2, SUF, 2))(jax.random.split(keys[4], N_GRP)).reshape((N_GRP, ROLLOUTS)).astype(jnp.int32)
    new_latent = draw_new_latent(jax.random.fold_in(keys[14], 71), 0)
    w_uv = scatter_about(keys[6], (HEADS, LAT, NOPE), LAT ** -0.5, 0.25, ((0, 32),))
    w_out = scatter_about(keys[7], (HEADS, NOPE, D), (HEADS * NOPE // 16) ** -0.5, 0.25, ((0, 32),))
    ffn_gain = jnp.clip(1.0 + 0.18 * jax.random.normal(keys[8], (D,), jnp.float32), 0.099609375, 1.8984375).astype(jnp.bfloat16)
    expert_ids_keys = jax.random.split(jax.random.fold_in(keys[9], 1), N_GRP * ROLLOUTS * STEPS // TOK_DEV)
    expert_ids_turns = jax.random.permutation(jax.random.fold_in(keys[9], 3), N_GRP * ROLLOUTS * STEPS // TOK_DEV)
    expert_ids = jax.vmap(lambda own, number: shared_out(jax.random.fold_in(keys[9], 2), own, number, TOK_DEV, EXPERTS, TOP, CAP, 2))(expert_ids_keys, expert_ids_turns).reshape((N_GRP, ROLLOUTS, STEPS, TOP))
    route_weights = jnp.clip(0.05 + 0.45 * jax.random.uniform(keys[10], (N_GRP, ROLLOUTS, STEPS, TOP), jnp.float32) ** shard_levels(keys[10], (N_GRP, ROLLOUTS, STEPS, TOP), ((0, 4), (1, 32)), -0.2, 0.2), 0.05, 0.5)
    w_gate = scatter_about(keys[11], (EXPERTS, D, FF), D ** -0.5, 0.09375, ((0, 128),))
    w_up = scatter_about(keys[12], (EXPERTS, D, FF), D ** -0.5, 0.09375, ((0, 128),))
    w_down = scatter_about(keys[13], (EXPERTS, FF, D), FF ** -0.5, 0.1875, ((0, 128),))
    return {"hidden": hidden, "query": query, "prefill_cache": prefill_cache, "suffix_cache": suffix_cache, "suffix_len": suffix_len, "new_latent": new_latent, "w_uv": w_uv, "w_out": w_out, "ffn_gain": ffn_gain, "expert_ids": expert_ids, "route_weights": route_weights, "w_gate": w_gate, "w_up": w_up, "w_down": w_down}


def attend(queries, prefix, own_cache, own_len, fresh):
    samples = queries.shape[0]
    key_width = LAT + ROPE
    query_rows = queries.reshape(samples, STEPS * HEADS, key_width).astype(jnp.float32)
    softmax_scale = (NOPE + ROPE) ** (-0.5)
    prefix_keys = prefix.astype(jnp.float32)
    own_keys = own_cache.astype(jnp.float32)
    fresh_keys = fresh.astype(jnp.float32)
    score_prefix = jnp.einsum('srl,kl->srk', query_rows, prefix_keys) * softmax_scale
    score_own = jnp.einsum('srl,skl->srk', query_rows, own_keys) * softmax_scale
    score_fresh = jnp.einsum('srl,stl->srt', query_rows, fresh_keys) * softmax_scale
    own_mask = jnp.arange(SUF, dtype=jnp.int32)[None, None, :] < own_len[:, None, None]
    row_step = jnp.arange(STEPS * HEADS, dtype=jnp.int32) // HEADS
    fresh_mask = (jnp.arange(STEPS, dtype=jnp.int32)[None, :] <= row_step[:, None])[None]
    score_own = jnp.where(own_mask, score_own, -jnp.inf)
    score_fresh = jnp.where(fresh_mask, score_fresh, -jnp.inf)
    rowmax = jnp.maximum(lax.optimization_barrier(jnp.max(score_prefix, -1)), jnp.maximum(lax.optimization_barrier(jnp.max(score_own, -1)), lax.optimization_barrier(jnp.max(score_fresh, -1))))[..., None]
    expo_prefix = jnp.exp(score_prefix - rowmax)
    expo_own = jnp.exp(score_own - rowmax)
    expo_fresh = jnp.exp(score_fresh - rowmax)
    denominator = lax.optimization_barrier(jnp.sum(expo_prefix, -1)) + lax.optimization_barrier(jnp.sum(expo_own, -1)) + lax.optimization_barrier(jnp.sum(expo_fresh, -1))
    rounded = lax.optimization_barrier((expo_prefix.astype(jnp.bfloat16), expo_own.astype(jnp.bfloat16), expo_fresh.astype(jnp.bfloat16)))
    weight_prefix = rounded[0].astype(jnp.float32)
    weight_own = rounded[1].astype(jnp.float32)
    weight_fresh = rounded[2].astype(jnp.float32)
    numerator = jnp.einsum('srk,kl->srl', weight_prefix, prefix_keys[:, :LAT])
    numerator = numerator + jnp.einsum('srk,skl->srl', weight_own, own_keys[:, :, :LAT])
    numerator = numerator + jnp.einsum('srt,stl->srl', weight_fresh, fresh_keys[:, :, :LAT])
    context = (numerator / denominator[..., None]).astype(jnp.bfloat16)
    return context.reshape(samples, STEPS, HEADS, LAT)

def expert_block(source, gate_matrix, up_matrix, down_matrix):
    gate_out = jnp.dot(source, gate_matrix, preferred_element_type=jnp.float32)
    up_out = jnp.dot(source, up_matrix, preferred_element_type=jnp.float32)
    middle = (jax.nn.silu(gate_out) * up_out).astype(jnp.bfloat16)
    return jnp.dot(middle, down_matrix, preferred_element_type=jnp.float32).astype(jnp.bfloat16)

def reference(hidden, query, prefill_cache, suffix_cache, suffix_len, new_latent, w_uv, w_out, ffn_gain, expert_ids, route_weights, w_gate, w_up, w_down):
    key_width = LAT + ROPE
    blocks = N_GRP * PROMPTS
    query_blocks = query.reshape(blocks, GROUP, STEPS, HEADS, key_width)
    prefix_blocks = prefill_cache.reshape(blocks, PREFIX, key_width)
    own_blocks = suffix_cache.reshape(blocks, GROUP, SUF, key_width)
    length_blocks = suffix_len.reshape(blocks, GROUP)
    fresh_blocks = new_latent.reshape(blocks, GROUP, STEPS, key_width)

    def prompt_output(operands):
        queries, prefix, own_cache, own_len, fresh = operands
        context = attend(queries, prefix, own_cache, own_len, fresh)
        head_value = jnp.einsum('sthl,hlv->sthv', context.astype(jnp.float32), w_uv.astype(jnp.float32)).astype(jnp.bfloat16)
        head_value = lax.optimization_barrier(head_value)
        return jnp.einsum('sthv,hvd->std', head_value.astype(jnp.float32), w_out.astype(jnp.float32))
    attention = lax.map(prompt_output, (query_blocks, prefix_blocks, own_blocks, length_blocks, fresh_blocks))
    attention = attention.reshape(N_GRP, ROLLOUTS, STEPS, D)
    residual = hidden.astype(jnp.float32) + attention
    mean_square = lax.optimization_barrier(jnp.mean(residual * residual, axis=-1, keepdims=True))
    normalized = (residual * lax.rsqrt(mean_square + 1e-06) * ffn_gain.astype(jnp.float32)).astype(jnp.bfloat16)
    token_rows = normalized.reshape(-1, D)
    route_flat = expert_ids.reshape(-1).astype(jnp.int32)
    route_count = route_flat.shape[0]
    budget = N_GRP * N_SMP * CAP

    def one_expert(routed_rows, expert_index):
        picked = jnp.nonzero(route_flat == expert_index, size=budget, fill_value=route_count)[0].astype(jnp.int32)
        source = token_rows[jnp.minimum(picked, route_count - 1) // TOP]
        result = expert_block(source, w_gate[expert_index], w_up[expert_index], w_down[expert_index])
        return (routed_rows.at[picked].set(result), None)
    routed_rows = lax.scan(one_expert, jnp.zeros((route_count + 1, D), jnp.bfloat16), jnp.arange(EXPERTS, dtype=jnp.int32))[0][:route_count]
    expert_rows = routed_rows.reshape(N_GRP, ROLLOUTS, STEPS, TOP, D).astype(jnp.float32)
    mixture = lax.optimization_barrier(jnp.sum(expert_rows * route_weights[..., None], axis=3))
    return (residual + mixture).astype(jnp.bfloat16)
```

```python
import jax
import jax.numpy as jnp
from jax import lax
from jax.experimental import pallas as pl
from jax.experimental.pallas import tpu as pltpu
from jax.sharding import PartitionSpec as P

D = 3584
HEADS = 64
LAT = 512
ROPE = 64
NOPE = 128
FF = 1024
TOP = 8
STEPS = 4
SUF = 128
TOK = 16
EXPERTS = 128
QTR = 4
WIDE = D // QTR
SCALE = (NOPE + ROPE) ** (-0.5)
F32 = jnp.float32
BF16 = jnp.bfloat16
VMEM_LIMIT = 56 * 1024 * 1024


def dot(a, b):
    return jnp.dot(a, b, preferred_element_type=F32)


def dot_t(a, b):
    return lax.dot_general(a, b, (((1,), (1,)), ((), ())), preferred_element_type=F32)


def iota(shape, dim):
    return lax.broadcasted_iota(jnp.int32, shape, dim)


def params():
    return pltpu.CompilerParams(vmem_limit_bytes=VMEM_LIMIT)


def attend_body(len_ref, q_ref, ka_ref, kb_ref, own_ref, fresh_ref, out_ref, held):
    s = pl.program_id(0)
    q = q_ref[0]
    rows = STEPS * HEADS
    keys = [ka_ref[...], kb_ref[...], own_ref[0], fresh_ref[0]]
    scores = [dot_t(q, k) for k in keys]
    scores[2] = jnp.where(iota((rows, SUF), 1) < len_ref[0, s], scores[2], -jnp.inf)
    step = iota((rows, STEPS), 0) // HEADS
    scores[3] = jnp.where(iota((rows, STEPS), 1) <= step, scores[3], -jnp.inf)
    top = jnp.max(scores[0], -1, keepdims=True)
    for sc in scores[1:]:
        top = jnp.maximum(top, jnp.max(sc, -1, keepdims=True))
    total = jnp.zeros((rows, 1), F32)
    acc = jnp.zeros((rows, LAT), F32)
    for sc, k in zip(scores, keys):
        p = jnp.exp((sc - top) * SCALE)
        total = total + jnp.sum(p, -1, keepdims=True)
        acc = acc + dot(p.astype(BF16), k[:, :LAT])
    ctx = (acc / total).astype(BF16)
    for t in range(STEPS):
        held[s * STEPS + t] = ctx[t * HEADS : (t + 1) * HEADS]

    @pl.when(s == pl.num_programs(0) - 1)
    def _():
        n = TOK * 16
        perm = (iota((n, n), 1) == (iota((n, n), 0) % TOK) * 16 + iota((n, n), 0) // TOK).astype(BF16)
        for b in range(HEADS // 16):
            part = held[:, b * 16 : (b + 1) * 16, :].reshape(n, LAT)
            out_ref[b * 16 : (b + 1) * 16] = dot(perm, part).astype(BF16).reshape(16, TOK, LAT)


def attend(lens, q, ka, kb, own, fresh):
    samples, rows, width = q.shape
    half = ka.shape[0]
    return pl.pallas_call(
        attend_body,
        grid=(samples,),
        in_specs=[
            pl.BlockSpec(memory_space=pltpu.SMEM),
            pl.BlockSpec((1, rows, width), lambda i: (i, 0, 0)),
            pl.BlockSpec((half, width), lambda i: (0, 0)),
            pl.BlockSpec((half, width), lambda i: (0, 0)),
            pl.BlockSpec((1, SUF, width), lambda i: (i, 0, 0)),
            pl.BlockSpec((1, STEPS, width), lambda i: (i, 0, 0)),
        ],
        out_specs=pl.BlockSpec((HEADS, TOK, LAT), lambda i: (0, 0, 0)),
        out_shape=jax.ShapeDtypeStruct((HEADS, TOK, LAT), BF16),
        scratch_shapes=[pltpu.VMEM((TOK, HEADS, LAT), BF16)],
        compiler_params=params(),
        cost_estimate=pl.CostEstimate(
            flops=2 * samples * rows * (2 * half + SUF) * (width + LAT),
            bytes_accessed=8 * 1024 * 1024,
            transcendentals=samples * rows * (2 * half + SUF),
        ),
        name="attend",
    )(lens, q, ka, kb, own, fresh)


def project_body(core_ref, x_ref, uva_ref, uvb_ref, oa_ref, ob_ref, out_ref, hv):
    chips, _, tok, _ = x_ref.shape
    rows = chips * tok

    @pl.when(pl.program_id(0) == 0)
    def _():
        core = core_ref[0]
        for side, uv in enumerate((uva_ref, uvb_ref)):
            first = 2 * core if side == 0 else 2 * (1 - core)
            for h in range(2):
                xh = x_ref[:, pl.ds(first + h, 1)].reshape(rows, LAT)
                hv[side, :, h * NOPE : (h + 1) * NOPE] = dot(xh, uv[h]).astype(BF16)

    width = out_ref.shape[-1]
    y = dot(hv[0], oa_ref[...].reshape(2 * NOPE, width)) + dot(hv[1], ob_ref[...].reshape(2 * NOPE, width))
    out_ref[...] = y.astype(BF16).reshape(chips, tok, width)


def project(core, x, uva, uvb, oa, ob):
    chips, _, tok, _ = x.shape
    whole = lambda shape: pl.BlockSpec(shape, lambda i: (0,) * len(shape))
    cols = lambda shape: pl.BlockSpec(shape, lambda i: (0, 0, i))
    return pl.pallas_call(
        project_body,
        grid=(QTR,),
        in_specs=[
            pl.BlockSpec(memory_space=pltpu.SMEM),
            whole(x.shape),
            whole(uva.shape),
            whole(uvb.shape),
            cols((2, NOPE, WIDE)),
            cols((2, NOPE, WIDE)),
        ],
        out_specs=cols((chips, tok, WIDE)),
        out_shape=jax.ShapeDtypeStruct((chips, tok, D), BF16),
        scratch_shapes=[pltpu.VMEM((2, chips * tok, 2 * NOPE), BF16)],
        compiler_params=params(),
        cost_estimate=pl.CostEstimate(flops=1100000000, bytes_accessed=7 * 1024 * 1024, transcendentals=0),
        name="project",
    )(core, x, uva, uvb, oa, ob)


def route_body(ids_ref, w_ref, send_ref, mix_ref):
    lines = EXPERTS * 2 * QTR
    ids = ids_ref[...]
    w = w_ref[...]
    lane = iota((TOK, EXPERTS), 1)
    named = jnp.zeros((TOK, EXPERTS), F32)
    weight = jnp.zeros((TOK, EXPERTS), F32)
    for k in range(TOP):
        hit = ids[:, k : k + 1] == lane
        named = named + jnp.where(hit, 1.0, 0.0)
        weight = weight + jnp.where(hit, w[:, k : k + 1], 0.0)
    below = (iota((TOK, TOK), 1) < iota((TOK, TOK), 0)).astype(BF16)
    earlier = dot(below, named.astype(BF16))
    spread = (iota((EXPERTS, lines), 1) // (2 * QTR) == iota((EXPERTS, lines), 0)).astype(BF16)
    high = weight.astype(BF16)
    low = (weight - high.astype(F32)).astype(BF16)
    stack = jnp.concatenate([named.astype(BF16), earlier.astype(BF16), high, low], axis=0)
    wide = dot(stack, spread)
    named, earlier, high, low = (wide[i * TOK : (i + 1) * TOK] for i in range(4))
    col = iota((TOK, lines), 1)
    slot = (col % (2 * QTR)) // QTR
    chosen = jnp.logical_and(named > 0.5, jnp.abs(earlier - slot.astype(F32)) < 0.5)
    sel = []
    for q in range(QTR):
        here = jnp.logical_and(chosen, col % QTR == q)
        sel.append(jnp.where(here, 1.0, 0.0))
        mix_ref[q * TOK : (q + 1) * TOK, :] = jnp.where(here, high, 0.0).astype(BF16)
        mix_ref[(QTR + q) * TOK : (QTR + q + 1) * TOK, :] = jnp.where(here, low, 0.0).astype(BF16)
    send_ref[...] = jnp.concatenate(sel, axis=0).T.astype(BF16)


def route(ids, w):
    lines = EXPERTS * 2 * QTR
    return pl.pallas_call(
        route_body,
        out_shape=(
            jax.ShapeDtypeStruct((lines, QTR * TOK), BF16),
            jax.ShapeDtypeStruct((2 * QTR * TOK, lines), BF16),
        ),
        compiler_params=params(),
        name="route",
    )(ids, w)


def dispatch_body(parts_ref, hid_ref, gain_ref, send_ref, res_ref, out_ref):
    total = parts_ref[0].astype(F32)
    for i in range(1, parts_ref.shape[0]):
        total = total + parts_ref[i].astype(F32)
    residual = hid_ref[...].astype(F32) + total
    res_ref[...] = residual
    mean = jnp.mean(residual * residual, axis=-1, keepdims=True)
    norm = (residual * lax.rsqrt(mean + 1e-06) * gain_ref[...].astype(F32)).astype(BF16)
    tall = jnp.concatenate([norm[:, q * WIDE : (q + 1) * WIDE] for q in range(QTR)], axis=0)
    out_ref[...] = dot(send_ref[...], tall).astype(BF16)


def dispatch(parts, hid, gain, send):
    return pl.pallas_call(
        dispatch_body,
        out_shape=(
            jax.ShapeDtypeStruct((TOK, D), F32),
            jax.ShapeDtypeStruct((send.shape[0], WIDE), BF16),
        ),
        compiler_params=params(),
        name="dispatch",
    )(parts, hid, gain, send)


def expert_body(x_hbm, wg_hbm, wu_hbm, wd_hbm, out_hbm, x, wg, wu, wd, mid, res, back, sems, xsem, osem):
    lines = x.shape[0]
    rows = lines // QTR
    group = rows // 4
    load_x = pltpu.make_async_copy(x_hbm, x, xsem)
    load_x.start()
    loads_g, loads_u, loads_d = [], [], []
    for q in range(QTR):
        span = pl.ds(q * WIDE, WIDE)
        loads_g.append(pltpu.make_async_copy(wg_hbm.at[0, span, :], wg.at[span, :], sems.at[0, q]))
        loads_u.append(pltpu.make_async_copy(wu_hbm.at[0, span, :], wu.at[span, :], sems.at[1, q]))
        loads_d.append(pltpu.make_async_copy(wd_hbm.at[0, :, span], wd.at[:, span], sems.at[2, q]))
    for q in range(QTR):
        loads_g[q].start()
        loads_u[q].start()
    for q in range(QTR):
        loads_d[q].start()
    n = lines // 4
    out_row, in_row = iota((n, n), 0), iota((n, n), 1)
    perm = (in_row == (out_row % group) * QTR + out_row // group).astype(BF16)
    unperm = (out_row == (in_row % group) * QTR + in_row // group).astype(BF16)
    load_x.wait()
    sorted_rows = [dot(perm, x[i * n : (i + 1) * n, :]).astype(BF16) for i in range(4)]
    gate = jnp.zeros((rows, FF), F32)
    up = jnp.zeros((rows, FF), F32)
    for q in range(QTR):
        xq = jnp.concatenate([r[q * group : (q + 1) * group] for r in sorted_rows], axis=0)
        span = pl.ds(q * WIDE, WIDE)
        loads_g[q].wait()
        gate = gate + dot(xq, wg[span, :])
        loads_u[q].wait()
        up = up + dot(xq, wu[span, :])
    mid[...] = (gate / (1.0 + jnp.exp(-gate)) * up).astype(BF16)
    for q in range(QTR):
        loads_d[q].wait()
        res[q] = dot(mid[...], wd[:, q * WIDE : (q + 1) * WIDE]).astype(BF16)
    stores = []
    for i in range(4):
        part = res[:, i * group : (i + 1) * group, :].reshape(n, WIDE)
        back[i * n : (i + 1) * n, :] = dot(unperm, part).astype(BF16)
        stores.append(
            pltpu.make_async_copy(back.at[i * n : (i + 1) * n, :], out_hbm.at[i * n : (i + 1) * n, :], osem.at[i])
        )
        stores[-1].start()
    for st in stores:
        st.wait()


def expert(x, wg, wu, wd):
    lines = x.shape[0]
    hbm = pl.BlockSpec(memory_space=pl.ANY)
    return pl.pallas_call(
        expert_body,
        in_specs=[hbm] * 4,
        out_specs=hbm,
        out_shape=jax.ShapeDtypeStruct(x.shape, BF16),
        scratch_shapes=[
            pltpu.VMEM(x.shape, BF16),
            pltpu.VMEM((D, FF), BF16),
            pltpu.VMEM((D, FF), BF16),
            pltpu.VMEM((FF, D), BF16),
            pltpu.VMEM((lines // QTR, FF), BF16),
            pltpu.VMEM((QTR, lines // QTR, WIDE), BF16),
            pltpu.VMEM(x.shape, BF16),
            pltpu.SemaphoreType.DMA((3, QTR)),
            pltpu.SemaphoreType.DMA,
            pltpu.SemaphoreType.DMA((4,)),
        ],
        compiler_params=params(),
        cost_estimate=pl.CostEstimate(
            flops=6 * (lines // QTR) * D * FF, bytes_accessed=26 * 1024 * 1024, transcendentals=lines * FF // QTR
        ),
        name="expert",
    )(x, wg, wu, wd)


def combine_body(mix_ref, back_ref, res_ref, out_ref):
    both = dot(mix_ref[...], back_ref[...])
    n = QTR * TOK
    y = both[:n] + both[n:]
    for q in range(QTR):
        span = slice(q * WIDE, (q + 1) * WIDE)
        out_ref[:, span] = (res_ref[:, span] + y[q * TOK : (q + 1) * TOK]).astype(BF16)


def combine(mix, back, res):
    return pl.pallas_call(
        combine_body,
        out_shape=jax.ShapeDtypeStruct((TOK, D), BF16),
        compiler_params=params(),
        name="combine",
    )(mix, back, res)


def on_device(
    hidden,
    query,
    prefill_cache,
    suffix_cache,
    suffix_len,
    new_latent,
    w_uv,
    w_out,
    ffn_gain,
    expert_ids,
    route_weights,
    w_gate,
    w_up,
    w_down,
):
    samples = query.shape[1]
    n_smp = lax.axis_size("smp")
    chips = n_smp // 2
    prompts, span, width = prefill_cache.shape[1:]
    core = lax.axis_index("smp") % 2
    pair = [(i, i ^ 1) for i in range(n_smp)]
    same_core = [[2 * k + c for k in range(chips)] for c in range(2)]

    shared = n_smp // prompts // 2
    slab = prefill_cache[0].reshape(prompts, 1, 2, span // 2, width)
    outgoing = jnp.broadcast_to(slab, (prompts, shared, 2, span // 2, width)).reshape(n_smp, span // 2, width)
    half_a = lax.all_to_all(outgoing, "smp", 0, 0, tiled=True).reshape(-1, width)
    half_b = lax.ppermute(half_a, "smp", pair)

    uv_b = lax.ppermute(w_uv, "smp", pair)
    out_b = lax.ppermute(w_out, "smp", pair)
    send, mix = route(expert_ids.reshape(TOK, TOP), route_weights.reshape(TOK, TOP))

    context = attend(
        suffix_len, query.reshape(samples, STEPS * HEADS, width), half_a, half_b, suffix_cache[0], new_latent[0]
    )
    by_chip = context.reshape(chips, HEADS // chips, TOK, LAT)
    by_heads = lax.all_to_all(by_chip, "smp", 0, 0, tiled=True, axis_index_groups=same_core)
    shares = project(core.reshape(1), by_heads, w_uv, uv_b, w_out, out_b)
    parts = lax.all_to_all(shares, "smp", 0, 0, tiled=True, axis_index_groups=same_core)
    residual, rows = dispatch(parts, hidden.reshape(TOK, D), ffn_gain.reshape(1, D), send)

    rows = rows.reshape(EXPERTS, 2 * QTR, WIDE)
    arrived = lax.all_to_all(rows, ("grp", "smp"), 0, 0, tiled=True)
    answered = expert(arrived.reshape(-1, WIDE), w_gate, w_up, w_down)
    answered = answered.reshape(EXPERTS, 2 * QTR, WIDE)
    returned = lax.all_to_all(answered, ("grp", "smp"), 0, 0, tiled=True)
    layer_out = combine(mix, returned.reshape(-1, WIDE), residual)
    return layer_out.reshape(hidden.shape)


def solution(mesh):
    placed = (
        P("grp", "smp", None, None),
        P("grp", "smp", None, None, None),
        P("grp", None, "smp", None),
        P("grp", "smp", None, None),
        P("grp", "smp"),
        P("grp", "smp", None, None),
        P("smp", None, None),
        P("smp", None, None),
        P(),
        P("grp", "smp", None, None),
        P("grp", "smp", None, None),
        P(("grp", "smp"), None, None),
        P(("grp", "smp"), None, None),
        P(("grp", "smp"), None, None),
    )
    return jax.shard_map(
        on_device,
        mesh=mesh,
        in_specs=placed,
        out_specs=P("grp", "smp", None, None),
        check_vma=False,
    )
```

```python
import jax
import jax.numpy as jnp
from jax import lax
from jax.experimental import pallas as pl
from jax.experimental.pallas import tpu as pltpu
from jax.sharding import PartitionSpec as P

D = 3584
HEADS = 64
LAT = 512
ROPE = 64
NOPE = 128
FF = 1024
TOP = 8
STEPS = 4
SUF = 128
TOK = 16
EXPERTS = 128
QTR = 4
WIDE = D // QTR
SCALE = (NOPE + ROPE) ** (-0.5)
F32 = jnp.float32
BF16 = jnp.bfloat16
MIB = 1024 * 1024


def dot(a, b):
    return jnp.dot(a, b, preferred_element_type=F32)


def dot_t(a, b):
    return lax.dot_general(a, b, (((1,), (1,)), ((), ())), preferred_element_type=F32)


def iota(shape, dim):
    return lax.broadcasted_iota(jnp.int32, shape, dim)


def params(mib):
    return pltpu.CompilerParams(vmem_limit_bytes=mib * MIB)


def attend_body(len_ref, q_ref, ka_ref, kb_ref, own_ref, fresh_ref, out_ref, held):
    s = pl.program_id(0)
    q = q_ref[0]
    rows = STEPS * HEADS
    scores = [dot_t(q, ka_ref[...]), dot_t(q, kb_ref[...]), dot(q, own_ref[0]), dot_t(q, fresh_ref[0])]
    scores[2] = jnp.where(iota((rows, SUF), 1) < len_ref[0, s], scores[2], -jnp.inf)
    step = iota((rows, STEPS), 0) // HEADS
    scores[3] = jnp.where(iota((rows, STEPS), 1) <= step, scores[3], -jnp.inf)
    top = jnp.max(scores[0], -1, keepdims=True)
    for sc in scores[1:]:
        top = jnp.maximum(top, jnp.max(sc, -1, keepdims=True))
    total = jnp.zeros((rows, 1), F32)
    acc = jnp.zeros((rows, LAT), F32)
    for i, sc in enumerate(scores):
        p = jnp.exp((sc - top) * SCALE)
        total = total + jnp.sum(p, -1, keepdims=True)
        p = p.astype(BF16)
        if i == 2:
            acc = acc + dot_t(p, own_ref[0, :LAT, :])
        else:
            acc = acc + dot(p, (ka_ref, kb_ref, None, fresh_ref.at[0])[i][:, :LAT])
    ctx = (acc / total).astype(BF16)
    for t in range(STEPS):
        held[s * STEPS + t] = ctx[t * HEADS : (t + 1) * HEADS]

    @pl.when(s == pl.num_programs(0) - 1)
    def _():
        n = TOK * 16
        perm = (iota((n, n), 1) == (iota((n, n), 0) % TOK) * 16 + iota((n, n), 0) // TOK).astype(BF16)
        for b in range(HEADS // 16):
            part = held[:, b * 16 : (b + 1) * 16, :].reshape(n, LAT)
            out_ref[b * 16 : (b + 1) * 16] = dot(perm, part).astype(BF16).reshape(16, TOK, LAT)


def attend(lens, q, ka, kb, own, fresh):
    samples, rows, width = q.shape
    half = ka.shape[0]
    return pl.pallas_call(
        attend_body,
        grid=(samples,),
        in_specs=[
            pl.BlockSpec(memory_space=pltpu.SMEM),
            pl.BlockSpec((1, rows, width), lambda i: (i, 0, 0)),
            pl.BlockSpec((half, width), lambda i: (0, 0)),
            pl.BlockSpec((half, width), lambda i: (0, 0)),
            pl.BlockSpec((1, width, SUF), lambda i: (i, 0, 0)),
            pl.BlockSpec((1, STEPS, width), lambda i: (i, 0, 0)),
        ],
        out_specs=pl.BlockSpec((HEADS, TOK, LAT), lambda i: (0, 0, 0)),
        out_shape=jax.ShapeDtypeStruct((HEADS, TOK, LAT), BF16),
        scratch_shapes=[pltpu.VMEM((TOK, HEADS, LAT), BF16)],
        compiler_params=params(28),
        cost_estimate=pl.CostEstimate(
            flops=2 * samples * rows * (2 * half + SUF) * (width + LAT),
            bytes_accessed=8 * 1024 * 1024,
            transcendentals=samples * rows * (2 * half + SUF),
        ),
        name="attend",
    )(lens, q, ka, kb, own, fresh)


def project_body(core_ref, x_ref, uva_ref, uvb_ref, oa_ref, ob_ref, out_ref, hv):
    chips, _, tok, _ = x_ref.shape
    rows = chips * tok

    @pl.when(pl.program_id(0) == 0)
    def _():
        core = core_ref[0]
        for side, uv in enumerate((uva_ref, uvb_ref)):
            first = 2 * core if side == 0 else 2 * (1 - core)
            for h in range(2):
                xh = x_ref[:, pl.ds(first + h, 1)].reshape(rows, LAT)
                hv[side, :, h * NOPE : (h + 1) * NOPE] = dot(xh, uv[h]).astype(BF16)

    width = out_ref.shape[-1]
    y = dot(hv[0], oa_ref[...].reshape(2 * NOPE, width)) + dot(hv[1], ob_ref[...].reshape(2 * NOPE, width))
    out_ref[...] = y.astype(BF16).reshape(chips, tok, width)


def project(core, x, uva, uvb, oa, ob):
    chips, _, tok, _ = x.shape
    whole = lambda shape: pl.BlockSpec(shape, lambda i: (0,) * len(shape))
    cols = lambda shape: pl.BlockSpec(shape, lambda i: (0, 0, i))
    return pl.pallas_call(
        project_body,
        grid=(QTR,),
        in_specs=[
            pl.BlockSpec(memory_space=pltpu.SMEM),
            whole(x.shape),
            whole(uva.shape),
            whole(uvb.shape),
            cols((2, NOPE, WIDE)),
            cols((2, NOPE, WIDE)),
        ],
        out_specs=cols((chips, tok, WIDE)),
        out_shape=jax.ShapeDtypeStruct((chips, tok, D), BF16),
        scratch_shapes=[pltpu.VMEM((2, chips * tok, 2 * NOPE), BF16)],
        compiler_params=params(16),
        cost_estimate=pl.CostEstimate(flops=1100000000, bytes_accessed=7 * 1024 * 1024, transcendentals=0),
        name="project",
    )(core, x, uva, uvb, oa, ob)


def route_body(ids_ref, w_ref, send_ref, mix_ref):
    lines = EXPERTS * 2 * QTR
    ids = ids_ref[...]
    w = w_ref[...]
    lane = iota((TOK, EXPERTS), 1)
    named = jnp.zeros((TOK, EXPERTS), F32)
    weight = jnp.zeros((TOK, EXPERTS), F32)
    for k in range(TOP):
        hit = ids[:, k : k + 1] == lane
        named = named + jnp.where(hit, 1.0, 0.0)
        weight = weight + jnp.where(hit, w[:, k : k + 1], 0.0)
    below = (iota((TOK, TOK), 1) < iota((TOK, TOK), 0)).astype(BF16)
    earlier = dot(below, named.astype(BF16))
    spread = (iota((EXPERTS, lines), 1) // (2 * QTR) == iota((EXPERTS, lines), 0)).astype(BF16)
    high = weight.astype(BF16)
    low = (weight - high.astype(F32)).astype(BF16)
    stack = jnp.concatenate([named.astype(BF16), earlier.astype(BF16), high, low], axis=0)
    wide = dot(stack, spread)
    named, earlier, high, low = (wide[i * TOK : (i + 1) * TOK] for i in range(4))
    col = iota((TOK, lines), 1)
    slot = (col % (2 * QTR)) // QTR
    chosen = jnp.logical_and(named > 0.5, jnp.abs(earlier - slot.astype(F32)) < 0.5)
    sel = []
    for q in range(QTR):
        here = jnp.logical_and(chosen, col % QTR == q)
        sel.append(jnp.where(here, 1.0, 0.0))
        mix_ref[q * TOK : (q + 1) * TOK, :] = jnp.where(here, high, 0.0).astype(BF16)
        mix_ref[(QTR + q) * TOK : (QTR + q + 1) * TOK, :] = jnp.where(here, low, 0.0).astype(BF16)
    send_ref[...] = jnp.concatenate(sel, axis=0).T.astype(BF16)


def route(ids, w):
    lines = EXPERTS * 2 * QTR
    return pl.pallas_call(
        route_body,
        out_shape=(
            jax.ShapeDtypeStruct((lines, QTR * TOK), BF16),
            jax.ShapeDtypeStruct((2 * QTR * TOK, lines), BF16),
        ),
        compiler_params=params(8),
        name="route",
    )(ids, w)


def dispatch_body(parts_ref, hid_ref, gain_ref, send_ref, res_ref, out_ref):
    total = parts_ref[0].astype(F32)
    for i in range(1, parts_ref.shape[0]):
        total = total + parts_ref[i].astype(F32)
    residual = hid_ref[...].reshape(TOK, D).astype(F32) + total
    res_ref[...] = residual
    mean = jnp.mean(residual * residual, axis=-1, keepdims=True)
    norm = (residual * lax.rsqrt(mean + 1e-06) * gain_ref[...].astype(F32)).astype(BF16)
    tall = jnp.concatenate([norm[:, q * WIDE : (q + 1) * WIDE] for q in range(QTR)], axis=0)
    out_ref[...] = dot(send_ref[...], tall).astype(BF16)


def dispatch(parts, hid, gain, send):
    return pl.pallas_call(
        dispatch_body,
        out_shape=(
            jax.ShapeDtypeStruct((TOK, D), F32),
            jax.ShapeDtypeStruct((send.shape[0], WIDE), BF16),
        ),
        compiler_params=params(14),
        name="dispatch",
    )(parts, hid, gain, send)


CHUNK = 512
PIECES = D // CHUNK
FLYING = 6


def expert_body(x_hbm, wg_hbm, wu_hbm, wd_hbm, out_hbm, x, xs, wg, wu, wd, mid, res, back, sems, xsem, osem):
    lines = x.shape[0]
    rows = lines // QTR
    group = rows // 4
    loads = []
    for c in range(PIECES):
        span = pl.ds(c * CHUNK, CHUNK)
        loads.append(pltpu.make_async_copy(wg_hbm.at[0, span, :], wg.at[span, :], sems.at[2 * c]))
        loads.append(pltpu.make_async_copy(wu_hbm.at[0, span, :], wu.at[span, :], sems.at[2 * c + 1]))
    for c in range(PIECES):
        span = pl.ds(c * CHUNK, CHUNK)
        loads.append(pltpu.make_async_copy(wd_hbm.at[0, :, span], wd.at[:, span], sems.at[2 * PIECES + c]))
    load_x = pltpu.make_async_copy(x_hbm, x, xsem)
    load_x.start()
    for i in range(FLYING):
        loads[i].start()

    def take(i):
        loads[i].wait()
        if i + FLYING < len(loads):
            loads[i + FLYING].start()

    n = lines // 4
    out_row, in_row = iota((n, n), 0), iota((n, n), 1)
    perm = (in_row == (out_row % group) * QTR + out_row // group).astype(BF16)
    unperm = (out_row == (in_row % group) * QTR + in_row // group).astype(BF16)
    load_x.wait()
    for i in range(4):
        part = dot(perm, x[i * n : (i + 1) * n, :]).astype(BF16)
        for q in range(QTR):
            xs[i * group : (i + 1) * group, q * WIDE : (q + 1) * WIDE] = part[q * group : (q + 1) * group]
    gate = jnp.zeros((rows, FF), F32)
    up = jnp.zeros((rows, FF), F32)
    for c in range(PIECES):
        xc = xs[:, c * CHUNK : (c + 1) * CHUNK]
        take(2 * c)
        gate = gate + dot(xc, wg[c * CHUNK : (c + 1) * CHUNK, :])
        take(2 * c + 1)
        up = up + dot(xc, wu[c * CHUNK : (c + 1) * CHUNK, :])
    mid[...] = (gate / (1.0 + jnp.exp(-gate)) * up).astype(BF16)
    for c in range(PIECES):
        take(2 * PIECES + c)
        res[:, c * CHUNK : (c + 1) * CHUNK] = dot(mid[...], wd[:, c * CHUNK : (c + 1) * CHUNK]).astype(BF16)
    stores = []
    for i in range(4):
        part = [res[i * group : (i + 1) * group, q * WIDE : (q + 1) * WIDE] for q in range(QTR)]
        back[i * n : (i + 1) * n, :] = dot(unperm, jnp.concatenate(part, axis=0)).astype(BF16)
        stores.append(
            pltpu.make_async_copy(back.at[i * n : (i + 1) * n, :], out_hbm.at[i * n : (i + 1) * n, :], osem.at[i])
        )
        stores[-1].start()
    for st in stores:
        st.wait()


def expert(x, wg, wu, wd):
    lines = x.shape[0]
    rows = lines // QTR
    hbm = pl.BlockSpec(memory_space=pl.ANY)
    return pl.pallas_call(
        expert_body,
        in_specs=[hbm] * 4,
        out_specs=hbm,
        out_shape=jax.ShapeDtypeStruct(x.shape, BF16),
        scratch_shapes=[
            pltpu.VMEM(x.shape, BF16),
            pltpu.VMEM((rows, D), BF16),
            pltpu.VMEM((D, FF), BF16),
            pltpu.VMEM((D, FF), BF16),
            pltpu.VMEM((FF, D), BF16),
            pltpu.VMEM((rows, FF), BF16),
            pltpu.VMEM((rows, D), BF16),
            pltpu.VMEM(x.shape, BF16),
            pltpu.SemaphoreType.DMA((3 * PIECES,)),
            pltpu.SemaphoreType.DMA,
            pltpu.SemaphoreType.DMA((4,)),
        ],
        compiler_params=params(44),
        cost_estimate=pl.CostEstimate(
            flops=6 * rows * D * FF, bytes_accessed=26 * 1024 * 1024, transcendentals=rows * FF
        ),
        name="expert",
    )(x, wg, wu, wd)


def combine_body(mix_ref, back_ref, res_ref, out_ref):
    both = dot(mix_ref[...], back_ref[...])
    n = QTR * TOK
    y = both[:n] + both[n:]
    for q in range(QTR):
        span = slice(q * WIDE, (q + 1) * WIDE)
        z = (res_ref[:, span] + y[q * TOK : (q + 1) * TOK]).astype(BF16)
        for s in range(TOK // STEPS):
            out_ref[0, s, :, span] = z[s * STEPS : (s + 1) * STEPS]


def combine(mix, back, res):
    return pl.pallas_call(
        combine_body,
        out_shape=jax.ShapeDtypeStruct((1, TOK // STEPS, STEPS, D), BF16),
        compiler_params=params(10),
        name="combine",
    )(mix, back, res)


def on_device(
    hidden,
    query,
    prefill_cache,
    suffix_cache,
    suffix_len,
    new_latent,
    w_uv,
    w_out,
    ffn_gain,
    expert_ids,
    route_weights,
    w_gate,
    w_up,
    w_down,
):
    samples = query.shape[1]
    n_smp = lax.axis_size("smp")
    chips = n_smp // 2
    prompts, span, width = prefill_cache.shape[1:]
    core = lax.axis_index("smp") % 2
    pair = [(i, i ^ 1) for i in range(n_smp)]
    same_core = [[2 * k + c for k in range(chips)] for c in range(2)]

    shared = n_smp // prompts // 2
    slab = prefill_cache[0].reshape(prompts, 1, 2, span // 2, width)
    outgoing = jnp.broadcast_to(slab, (prompts, shared, 2, span // 2, width)).reshape(n_smp, span // 2, width)
    half_a = lax.all_to_all(outgoing, "smp", 0, 0, tiled=True)
    half_b = lax.ppermute(half_a, "smp", pair).reshape(-1, width)
    half_a = half_a.reshape(-1, width)
    own = jnp.swapaxes(suffix_cache[0], 1, 2)

    uv_b = lax.ppermute(w_uv, "smp", pair)
    out_b = lax.ppermute(w_out, "smp", pair)
    send, mix = route(expert_ids.reshape(TOK, TOP), route_weights.reshape(TOK, TOP))

    context = attend(
        suffix_len, query.reshape(samples, STEPS * HEADS, width), half_a, half_b, own, new_latent[0]
    )
    by_chip = context.reshape(chips, HEADS // chips, TOK, LAT)
    by_heads = lax.all_to_all(by_chip, "smp", 0, 0, tiled=True, axis_index_groups=same_core)
    shares = project(core.reshape(1), by_heads, w_uv, uv_b, w_out, out_b)
    parts = lax.all_to_all(shares, "smp", 0, 0, tiled=True, axis_index_groups=same_core)
    residual, rows = dispatch(parts, hidden[0], ffn_gain.reshape(1, D), send)

    rows = rows.reshape(EXPERTS, 2 * QTR, WIDE)
    arrived = lax.all_to_all(rows, ("grp", "smp"), 0, 0, tiled=True)
    answered = expert(arrived.reshape(-1, WIDE), w_gate, w_up, w_down)
    answered = answered.reshape(EXPERTS, 2 * QTR, WIDE)
    returned = lax.all_to_all(answered, ("grp", "smp"), 0, 0, tiled=True)
    return combine(mix, returned.reshape(-1, WIDE), residual)


def solution(mesh):
    placed = (
        P("grp", "smp", None, None),
        P("grp", "smp", None, None, None),
        P("grp", None, "smp", None),
        P("grp", "smp", None, None),
        P("grp", "smp"),
        P("grp", "smp", None, None),
        P("smp", None, None),
        P("smp", None, None),
        P(),
        P("grp", "smp", None, None),
        P("grp", "smp", None, None),
        P(("grp", "smp"), None, None),
        P(("grp", "smp"), None, None),
        P(("grp", "smp"), None, None),
    )
    return jax.shard_map(
        on_device,
        mesh=mesh,
        in_specs=placed,
        out_specs=P("grp", "smp", None, None),
        check_vma=False,
    )
```

```python
import jax
import jax.numpy as jnp
from jax import lax
from jax.experimental import pallas as pl
from jax.experimental.pallas import tpu as pltpu
from jax.sharding import PartitionSpec as P

D = 3584
HEADS = 64
LAT = 512
ROPE = 64
NOPE = 128
FF = 1024
TOP = 8
STEPS = 4
SUF = 128
TOK = 16
EXPERTS = 128
QTR = 4
WIDE = D // QTR
SCALE = (NOPE + ROPE) ** (-0.5)
F32 = jnp.float32
BF16 = jnp.bfloat16
MIB = 1024 * 1024


def dot(a, b):
    return jnp.dot(a, b, preferred_element_type=F32)


def dot_t(a, b):
    return lax.dot_general(a, b, (((1,), (1,)), ((), ())), preferred_element_type=F32)


def iota(shape, dim):
    return lax.broadcasted_iota(jnp.int32, shape, dim)


def params(mib):
    return pltpu.CompilerParams(vmem_limit_bytes=mib * MIB)


def attend_body(len_ref, q_ref, ka_ref, kb_ref, own_ref, fresh_ref, out_ref, held):
    samples, rows, _ = q_ref.shape
    step = iota((rows, STEPS), 0) // HEADS
    causal = iota((rows, STEPS), 1) <= step
    slot = iota((rows, SUF), 1)

    def score(s):
        q = q_ref[s]
        own = jnp.where(slot < len_ref[0, s], dot(q, own_ref[s]), -jnp.inf)
        fresh = jnp.where(causal, dot_t(q, fresh_ref[s]), -jnp.inf)
        return [dot_t(q, ka_ref[...]), dot_t(q, kb_ref[...]), own, fresh]

    def settle(s, scores):
        top = jnp.max(scores[0], -1, keepdims=True)
        for sc in scores[1:]:
            top = jnp.maximum(top, jnp.max(sc, -1, keepdims=True))
        total = jnp.zeros((rows, 1), F32)
        acc = jnp.zeros((rows, LAT), F32)
        for i, sc in enumerate(scores):
            p = jnp.exp((sc - top) * SCALE)
            total = total + jnp.sum(p, -1, keepdims=True)
            p = p.astype(BF16)
            if i == 2:
                acc = acc + dot_t(p, own_ref[s, :LAT, :])
            else:
                acc = acc + dot(p, (ka_ref, kb_ref, None, fresh_ref.at[s])[i][:, :LAT])
        ctx = (acc / total).astype(BF16)
        for t in range(STEPS):
            held[s * STEPS + t] = ctx[t * HEADS : (t + 1) * HEADS]

    ahead = score(0)
    for s in range(samples):
        now = ahead
        if s + 1 < samples:
            ahead = score(s + 1)
        settle(s, now)
    n = TOK * 16
    perm = (iota((n, n), 1) == (iota((n, n), 0) % TOK) * 16 + iota((n, n), 0) // TOK).astype(BF16)
    for b in range(HEADS // 16):
        part = held[:, b * 16 : (b + 1) * 16, :].reshape(n, LAT)
        out_ref[b * 16 : (b + 1) * 16] = dot(perm, part).astype(BF16).reshape(16, TOK, LAT)


def attend(lens, q, ka, kb, own, fresh):
    samples, rows, width = q.shape
    half = ka.shape[0]
    vmem = pl.BlockSpec(memory_space=pltpu.VMEM)
    return pl.pallas_call(
        attend_body,
        in_specs=[pl.BlockSpec(memory_space=pltpu.SMEM)] + [vmem] * 5,
        out_specs=vmem,
        out_shape=jax.ShapeDtypeStruct((HEADS, TOK, LAT), BF16),
        scratch_shapes=[pltpu.VMEM((TOK, HEADS, LAT), BF16)],
        compiler_params=params(32),
        cost_estimate=pl.CostEstimate(
            flops=2 * samples * rows * (2 * half + SUF) * (width + LAT),
            bytes_accessed=8 * 1024 * 1024,
            transcendentals=samples * rows * (2 * half + SUF),
        ),
        name="attend",
    )(lens, q, ka, kb, own, fresh)


def project_body(core_ref, x_ref, uva_ref, uvb_ref, oa_ref, ob_ref, out_ref):
    chips, _, tok, _ = x_ref.shape
    rows = chips * tok
    core = core_ref[0]
    sides = []
    for side, uv in enumerate((uva_ref, uvb_ref)):
        first = 2 * core if side == 0 else 2 * (1 - core)
        cols = [dot(x_ref[:, pl.ds(first + h, 1)].reshape(rows, LAT), uv[h]).astype(BF16) for h in range(2)]
        sides.append(jnp.concatenate(cols, axis=1))
    both = jnp.concatenate(sides, axis=1)
    for c in range(D // 512):
        span = slice(c * 512, (c + 1) * 512)
        w = jnp.concatenate([o[:, :, span].reshape(2 * NOPE, 512) for o in (oa_ref, ob_ref)], axis=0)
        out_ref[:, :, span] = dot(both, w).astype(BF16).reshape(chips, tok, 512)


def project(core, x, uva, uvb, oa, ob):
    chips, _, tok, _ = x.shape
    vmem = pl.BlockSpec(memory_space=pltpu.VMEM)
    return pl.pallas_call(
        project_body,
        in_specs=[pl.BlockSpec(memory_space=pltpu.SMEM)] + [vmem] * 5,
        out_specs=vmem,
        out_shape=jax.ShapeDtypeStruct((chips, tok, D), BF16),
        compiler_params=params(20),
        cost_estimate=pl.CostEstimate(flops=1100000000, bytes_accessed=7 * 1024 * 1024, transcendentals=0),
        name="project",
    )(core, x, uva, uvb, oa, ob)


def route_body(ids_ref, w_ref, send_ref, mix_ref):
    lines = EXPERTS * 2 * QTR
    ids = ids_ref[...]
    w = w_ref[...]
    lane = iota((TOK, EXPERTS), 1)
    named = jnp.zeros((TOK, EXPERTS), F32)
    weight = jnp.zeros((TOK, EXPERTS), F32)
    for k in range(TOP):
        hit = ids[:, k : k + 1] == lane
        named = named + jnp.where(hit, 1.0, 0.0)
        weight = weight + jnp.where(hit, w[:, k : k + 1], 0.0)
    below = (iota((TOK, TOK), 1) < iota((TOK, TOK), 0)).astype(BF16)
    earlier = dot(below, named.astype(BF16))
    spread = (iota((EXPERTS, lines), 1) // (2 * QTR) == iota((EXPERTS, lines), 0)).astype(BF16)
    high = weight.astype(BF16)
    low = (weight - high.astype(F32)).astype(BF16)
    stack = jnp.concatenate([named.astype(BF16), earlier.astype(BF16), high, low], axis=0)
    wide = dot(stack, spread)
    named, earlier, high, low = (wide[i * TOK : (i + 1) * TOK] for i in range(4))
    col = iota((TOK, lines), 1)
    slot = (col % (2 * QTR)) // QTR
    chosen = jnp.logical_and(named > 0.5, jnp.abs(earlier - slot.astype(F32)) < 0.5)
    sel = []
    for q in range(QTR):
        here = jnp.logical_and(chosen, col % QTR == q)
        sel.append(jnp.where(here, 1.0, 0.0))
        mix_ref[q * TOK : (q + 1) * TOK, :] = jnp.where(here, high, 0.0).astype(BF16)
        mix_ref[(QTR + q) * TOK : (QTR + q + 1) * TOK, :] = jnp.where(here, low, 0.0).astype(BF16)
    send_ref[...] = jnp.concatenate(sel, axis=0).T.astype(BF16)


def route(ids, w):
    lines = EXPERTS * 2 * QTR
    return pl.pallas_call(
        route_body,
        out_shape=(
            jax.ShapeDtypeStruct((lines, QTR * TOK), BF16),
            jax.ShapeDtypeStruct((2 * QTR * TOK, lines), BF16),
        ),
        compiler_params=params(8),
        name="route",
    )(ids, w)


def dispatch_body(parts_ref, hid_ref, gain_ref, send_ref, res_ref, out_ref):
    total = parts_ref[0].astype(F32)
    for i in range(1, parts_ref.shape[0]):
        total = total + parts_ref[i].astype(F32)
    residual = hid_ref[...].reshape(TOK, D).astype(F32) + total
    res_ref[...] = residual
    mean = jnp.mean(residual * residual, axis=-1, keepdims=True)
    norm = (residual * lax.rsqrt(mean + 1e-06) * gain_ref[...].astype(F32)).astype(BF16)
    tall = jnp.concatenate([norm[:, q * WIDE : (q + 1) * WIDE] for q in range(QTR)], axis=0)
    out_ref[...] = dot(send_ref[...], tall).astype(BF16)


def dispatch(parts, hid, gain, send):
    return pl.pallas_call(
        dispatch_body,
        out_shape=(
            jax.ShapeDtypeStruct((TOK, D), F32),
            jax.ShapeDtypeStruct((send.shape[0], WIDE), BF16),
        ),
        compiler_params=params(14),
        name="dispatch",
    )(parts, hid, gain, send)


CHUNK = 512
PIECES = D // CHUNK
FLYING = 5


def expert_body(x, wg, wu, wd_hbm, out_ref, xs, wd, mid, res, sems):
    lines = x.shape[0]
    rows = lines // QTR
    group = rows // 4
    loads = []
    for c in range(PIECES):
        span = pl.ds(c * CHUNK, CHUNK)
        loads.append(pltpu.make_async_copy(wd_hbm.at[0, :, span], wd.at[:, span], sems.at[c]))
    for i in range(FLYING):
        loads[i].start()

    def take(i):
        loads[i].wait()
        if i + FLYING < len(loads):
            loads[i + FLYING].start()

    n = lines // 4
    out_row, in_row = iota((n, n), 0), iota((n, n), 1)
    perm = (in_row == (out_row % group) * QTR + out_row // group).astype(BF16)
    unperm = (out_row == (in_row % group) * QTR + in_row // group).astype(BF16)
    for i in range(4):
        part = dot(perm, x[i * n : (i + 1) * n, :]).astype(BF16)
        for q in range(QTR):
            xs[i * group : (i + 1) * group, q * WIDE : (q + 1) * WIDE] = part[q * group : (q + 1) * group]
    gate = dot(xs[...], wg[0])
    gate = gate / (1.0 + jnp.exp(-gate))
    up = dot(xs[...], wu[0])
    mid[...] = (gate * up).astype(BF16)
    for c in range(PIECES):
        take(c)
        span = slice(c * CHUNK, (c + 1) * CHUNK)
        res[:, span] = dot(mid[...], wd[:, span]).astype(BF16)
    for i in range(4):
        part = [res[i * group : (i + 1) * group, q * WIDE : (q + 1) * WIDE] for q in range(QTR)]
        out_ref[i * n : (i + 1) * n, :] = dot(unperm, jnp.concatenate(part, axis=0)).astype(BF16)


def expert(x, wg, wu, wd):
    lines = x.shape[0]
    rows = lines // QTR
    vmem = pl.BlockSpec(memory_space=pltpu.VMEM)
    hbm = pl.BlockSpec(memory_space=pl.ANY)
    return pl.pallas_call(
        expert_body,
        in_specs=[vmem, vmem, vmem, hbm],
        out_specs=vmem,
        out_shape=jax.ShapeDtypeStruct(x.shape, BF16),
        scratch_shapes=[
            pltpu.VMEM((rows, D), BF16),
            pltpu.VMEM((FF, D), BF16),
            pltpu.VMEM((rows, FF), BF16),
            pltpu.VMEM((rows, D), BF16),
            pltpu.SemaphoreType.DMA((PIECES,)),
        ],
        compiler_params=params(36),
        cost_estimate=pl.CostEstimate(
            flops=6 * rows * D * FF, bytes_accessed=26 * 1024 * 1024, transcendentals=rows * FF
        ),
        name="expert",
    )(x, wg, wu, wd)


def combine_body(mix_ref, back_ref, res_ref, out_ref):
    both = dot(mix_ref[...], back_ref[...])
    n = QTR * TOK
    y = both[:n] + both[n:]
    for q in range(QTR):
        span = slice(q * WIDE, (q + 1) * WIDE)
        z = (res_ref[:, span] + y[q * TOK : (q + 1) * TOK]).astype(BF16)
        for s in range(TOK // STEPS):
            out_ref[0, s, :, span] = z[s * STEPS : (s + 1) * STEPS]


def combine(mix, back, res):
    return pl.pallas_call(
        combine_body,
        out_shape=jax.ShapeDtypeStruct((1, TOK // STEPS, STEPS, D), BF16),
        compiler_params=params(10),
        name="combine",
    )(mix, back, res)


def on_device(
    hidden,
    query,
    prefill_cache,
    suffix_cache,
    suffix_len,
    new_latent,
    w_uv,
    w_out,
    ffn_gain,
    expert_ids,
    route_weights,
    w_gate,
    w_up,
    w_down,
):
    samples = query.shape[1]
    n_smp = lax.axis_size("smp")
    chips = n_smp // 2
    prompts, span, width = prefill_cache.shape[1:]
    core = lax.axis_index("smp") % 2
    pair = [(i, i ^ 1) for i in range(n_smp)]
    same_core = [[2 * k + c for k in range(chips)] for c in range(2)]

    shared = n_smp // prompts // 2
    slab = prefill_cache[0].reshape(prompts, 1, 2, span // 2, width)
    outgoing = jnp.broadcast_to(slab, (prompts, shared, 2, span // 2, width)).reshape(n_smp, span // 2, width)
    half_a = lax.all_to_all(outgoing, "smp", 0, 0, tiled=True)

    half_a, ids, weights, gain = lax.optimization_barrier((half_a, expert_ids, route_weights, ffn_gain))
    half_b = lax.ppermute(half_a, "smp", pair)
    send, mix = route(ids.reshape(TOK, TOP), weights.reshape(TOK, TOP))
    gain = gain.reshape(1, D)
    core = core.reshape(1)
    half_b, send, mix, gain, core, w_uv, w_out = lax.optimization_barrier(
        (half_b, send, mix, gain, core, w_uv, w_out)
    )
    uv_b = lax.ppermute(w_uv, "smp", pair)
    out_b = lax.ppermute(w_out, "smp", pair)
    half_a = half_a.reshape(-1, width)
    half_b = half_b.reshape(-1, width)
    own = jnp.swapaxes(suffix_cache[0], 1, 2)
    context = attend(
        suffix_len, query.reshape(samples, STEPS * HEADS, width), half_a, half_b, own, new_latent[0]
    )
    context, uv_b, out_b = lax.optimization_barrier((context, uv_b, out_b))
    by_chip = context.reshape(chips, HEADS // chips, TOK, LAT)
    by_heads = lax.all_to_all(by_chip, "smp", 0, 0, tiled=True, axis_index_groups=same_core)
    shares = project(core, by_heads, w_uv, uv_b, w_out, out_b)
    parts = lax.all_to_all(shares, "smp", 0, 0, tiled=True, axis_index_groups=same_core)
    residual, rows = dispatch(parts, hidden[0], gain, send)

    rows = rows.reshape(EXPERTS, 2 * QTR, WIDE)
    arrived = lax.all_to_all(rows, ("grp", "smp"), 0, 0, tiled=True)
    answered = expert(arrived.reshape(-1, WIDE), w_gate, w_up, w_down)
    answered = answered.reshape(EXPERTS, 2 * QTR, WIDE)
    returned = lax.all_to_all(answered, ("grp", "smp"), 0, 0, tiled=True)
    return combine(mix, returned.reshape(-1, WIDE), residual)


def solution(mesh):
    placed = (
        P("grp", "smp", None, None),
        P("grp", "smp", None, None, None),
        P("grp", None, "smp", None),
        P("grp", "smp", None, None),
        P("grp", "smp"),
        P("grp", "smp", None, None),
        P("smp", None, None),
        P("smp", None, None),
        P(),
        P("grp", "smp", None, None),
        P("grp", "smp", None, None),
        P(("grp", "smp"), None, None),
        P(("grp", "smp"), None, None),
        P(("grp", "smp"), None, None),
    )
    return jax.shard_map(
        on_device,
        mesh=mesh,
        in_specs=placed,
        out_specs=P("grp", "smp", None, None),
        check_vma=False,
    )
```

```python
import jax
import jax.numpy as jnp
from jax import lax
from jax.experimental import pallas as pl
from jax.experimental.pallas import tpu as pltpu
from jax.sharding import PartitionSpec as P

D = 3584
HEADS = 64
LAT = 512
ROPE = 64
NOPE = 128
FF = 1024
TOP = 8
STEPS = 4
SUF = 128
TOK = 16
EXPERTS = 128
QTR = 4
WIDE = D // QTR
SCALE = (NOPE + ROPE) ** (-0.5)
F32 = jnp.float32
BF16 = jnp.bfloat16
MIB = 1024 * 1024


def dot(a, b):
    return jnp.dot(a, b, preferred_element_type=F32)


def dot_t(a, b):
    return lax.dot_general(a, b, (((1,), (1,)), ((), ())), preferred_element_type=F32)


def iota(shape, dim):
    return lax.broadcasted_iota(jnp.int32, shape, dim)


def params(mib):
    return pltpu.CompilerParams(vmem_limit_bytes=mib * MIB)


SPAN = 32
LINES = SPAN * 4 + SPAN // 2
HALF = SPAN // 2


def pack_body(slab_ref, out_ref):
    prompts, span, _ = slab_ref.shape
    for p in range(prompts):
        for c in range(span // SPAN):
            x = slab_ref[p, c * SPAN : (c + 1) * SPAN, :]
            tiles = [x[:, i * 128 : (i + 1) * 128] for i in range(LAT // 128)]
            tiles.append(jnp.concatenate([x[:HALF, LAT:], x[HALF:, LAT:]], axis=1))
            block = jnp.concatenate(tiles, axis=0)
            for j in range(out_ref.shape[1]):
                out_ref[p, j, c] = block


def pack(slab, shared):
    prompts, span, _ = slab.shape
    vmem = pl.BlockSpec(memory_space=pltpu.VMEM)
    return pl.pallas_call(
        pack_body,
        in_specs=[vmem],
        out_specs=vmem,
        out_shape=jax.ShapeDtypeStruct((prompts, shared, span // SPAN, LINES, 128), BF16),
        compiler_params=params(8),
        name="pack",
    )(slab)


def latents(ref, g):
    tiles = [ref[:, i * SPAN + g * HALF : i * SPAN + (g + 1) * HALF, :] for i in range(LAT // 128)]
    return jnp.concatenate([t.reshape(-1, 128) for t in tiles], axis=1)


def keys(ref, g):
    return jnp.concatenate([latents(ref, g), ref[:, 4 * SPAN :, :].reshape(-1, 128)], axis=1)


def packed_scores(q, ref):
    gap = jnp.zeros((q.shape[0], ROPE), BF16)
    first = jnp.concatenate([q, gap], axis=1)
    second = jnp.concatenate([q[:, :LAT], gap, q[:, LAT:]], axis=1)
    return jnp.concatenate([dot_t(first, keys(ref, 0)), dot_t(second, keys(ref, 1))], axis=1)


def values(ref):
    return jnp.concatenate([latents(ref, 0), latents(ref, 1)], axis=0)


def score_body(len_ref, q_ref, ka_ref, own_ref, fresh_ref, sa_ref, so_ref, sf_ref):
    samples, rows, _ = q_ref.shape
    causal = iota((rows, STEPS), 1) <= iota((rows, STEPS), 0) // HEADS
    slot = iota((rows, SUF), 1)
    for s in range(samples):
        q = q_ref[s]
        sa_ref[s] = packed_scores(q, ka_ref)
        sf_ref[s] = jnp.where(causal, dot_t(q, fresh_ref[s]), -jnp.inf)
        so_ref[s] = jnp.where(slot < len_ref[0, s], dot(q, own_ref[s]), -jnp.inf)


def score(lens, q, ka, own, fresh):
    samples, rows, width = q.shape
    half = ka.shape[0] * SPAN
    vmem = pl.BlockSpec(memory_space=pltpu.VMEM)
    return pl.pallas_call(
        score_body,
        in_specs=[pl.BlockSpec(memory_space=pltpu.SMEM)] + [vmem] * 4,
        out_specs=[vmem] * 3,
        out_shape=(
            jax.ShapeDtypeStruct((samples, rows, half), F32),
            jax.ShapeDtypeStruct((samples, rows, SUF), F32),
            jax.ShapeDtypeStruct((samples, rows, STEPS), F32),
        ),
        compiler_params=params(18),
        cost_estimate=pl.CostEstimate(
            flops=2 * samples * rows * (half + SUF) * width, bytes_accessed=2 * 1024 * 1024, transcendentals=0
        ),
        name="score",
    )(lens, q, ka, own, fresh)


def attend_body(q_ref, own_ref, sa_ref, so_ref, sf_ref, ka_ref, kb_ref, fresh_ref, out_ref, held):
    samples, rows, _ = q_ref.shape

    def settle(s, ahead):
        scores = [sa_ref[s], ahead, so_ref[s], sf_ref[s]]
        top = jnp.max(scores[0], -1, keepdims=True)
        for sc in scores[1:]:
            top = jnp.maximum(top, jnp.max(sc, -1, keepdims=True))
        total = jnp.zeros((rows, 1), F32)
        acc = jnp.zeros((rows, LAT), F32)
        for i, sc in enumerate(scores):
            p = jnp.exp((sc - top) * SCALE)
            total = total + jnp.sum(p, -1, keepdims=True)
            p = p.astype(BF16)
            if i == 2:
                acc = acc + dot_t(p, own_ref[s, :LAT, :])
            elif i == 3:
                acc = acc + dot(p, fresh_ref[s, :, :LAT])
            else:
                acc = acc + dot(p, values((ka_ref, kb_ref)[i]))
        ctx = (acc / total).astype(BF16)
        for t in range(STEPS):
            held[s * STEPS + t] = ctx[t * HEADS : (t + 1) * HEADS]

    ahead = packed_scores(q_ref[0], kb_ref)
    for s in range(samples):
        now = ahead
        if s + 1 < samples:
            ahead = packed_scores(q_ref[s + 1], kb_ref)
        settle(s, now)
    n = TOK * 16
    perm = (iota((n, n), 1) == (iota((n, n), 0) % TOK) * 16 + iota((n, n), 0) // TOK).astype(BF16)
    for b in range(HEADS // 16):
        part = held[:, b * 16 : (b + 1) * 16, :].reshape(n, LAT)
        out_ref[b * 16 : (b + 1) * 16] = dot(perm, part).astype(BF16).reshape(16, TOK, LAT)


def attend(q, own, scored, ka, kb, fresh):
    samples, rows, width = q.shape
    half = ka.shape[0] * SPAN
    vmem = pl.BlockSpec(memory_space=pltpu.VMEM)
    return pl.pallas_call(
        attend_body,
        in_specs=[vmem] * 8,
        out_specs=vmem,
        out_shape=jax.ShapeDtypeStruct((HEADS, TOK, LAT), BF16),
        scratch_shapes=[pltpu.VMEM((TOK, HEADS, LAT), BF16)],
        compiler_params=params(30),
        cost_estimate=pl.CostEstimate(
            flops=2 * samples * rows * (half * width + (2 * half + SUF) * LAT),
            bytes_accessed=8 * 1024 * 1024,
            transcendentals=samples * rows * (2 * half + SUF),
        ),
        name="attend",
    )(q, own, *scored, ka, kb, fresh)


def project_body(core_ref, x_ref, uva_ref, uvb_ref, oa_ref, ob_ref, out_ref):
    chips, _, tok, _ = x_ref.shape
    rows = chips * tok
    core = core_ref[0]
    sides = []
    for side, uv in enumerate((uva_ref, uvb_ref)):
        first = 2 * core if side == 0 else 2 * (1 - core)
        cols = [dot(x_ref[:, pl.ds(first + h, 1)].reshape(rows, LAT), uv[h]).astype(BF16) for h in range(2)]
        sides.append(jnp.concatenate(cols, axis=1))
    both = jnp.concatenate(sides, axis=1)
    for c in range(D // 512):
        span = slice(c * 512, (c + 1) * 512)
        w = jnp.concatenate([o[:, :, span].reshape(2 * NOPE, 512) for o in (oa_ref, ob_ref)], axis=0)
        out_ref[:, :, span] = dot(both, w).astype(BF16).reshape(chips, tok, 512)


def project(core, x, uva, uvb, oa, ob):
    chips, _, tok, _ = x.shape
    vmem = pl.BlockSpec(memory_space=pltpu.VMEM)
    return pl.pallas_call(
        project_body,
        in_specs=[pl.BlockSpec(memory_space=pltpu.SMEM)] + [vmem] * 5,
        out_specs=vmem,
        out_shape=jax.ShapeDtypeStruct((chips, tok, D), BF16),
        compiler_params=params(20),
        cost_estimate=pl.CostEstimate(flops=1100000000, bytes_accessed=7 * 1024 * 1024, transcendentals=0),
        name="project",
    )(core, x, uva, uvb, oa, ob)


def route_body(ids_ref, w_ref, send_ref, mix_ref):
    lines = EXPERTS * 2 * QTR
    ids = ids_ref[...]
    w = w_ref[...]
    lane = iota((TOK, EXPERTS), 1)
    named = jnp.zeros((TOK, EXPERTS), F32)
    weight = jnp.zeros((TOK, EXPERTS), F32)
    for k in range(TOP):
        hit = ids[:, k : k + 1] == lane
        named = named + jnp.where(hit, 1.0, 0.0)
        weight = weight + jnp.where(hit, w[:, k : k + 1], 0.0)
    below = (iota((TOK, TOK), 1) < iota((TOK, TOK), 0)).astype(BF16)
    earlier = dot(below, named.astype(BF16))
    spread = (iota((EXPERTS, lines), 1) // (2 * QTR) == iota((EXPERTS, lines), 0)).astype(BF16)
    high = weight.astype(BF16)
    low = (weight - high.astype(F32)).astype(BF16)
    stack = jnp.concatenate([named.astype(BF16), earlier.astype(BF16), high, low], axis=0)
    wide = dot(stack, spread)
    named, earlier, high, low = (wide[i * TOK : (i + 1) * TOK] for i in range(4))
    col = iota((TOK, lines), 1)
    slot = (col % (2 * QTR)) // QTR
    chosen = jnp.logical_and(named > 0.5, jnp.abs(earlier - slot.astype(F32)) < 0.5)
    sel = []
    for q in range(QTR):
        here = jnp.logical_and(chosen, col % QTR == q)
        sel.append(jnp.where(here, 1.0, 0.0))
        mix_ref[q * TOK : (q + 1) * TOK, :] = jnp.where(here, high, 0.0).astype(BF16)
        mix_ref[(QTR + q) * TOK : (QTR + q + 1) * TOK, :] = jnp.where(here, low, 0.0).astype(BF16)
    send_ref[...] = jnp.concatenate(sel, axis=0).T.astype(BF16)


def route(ids, w):
    lines = EXPERTS * 2 * QTR
    return pl.pallas_call(
        route_body,
        out_shape=(
            jax.ShapeDtypeStruct((lines, QTR * TOK), BF16),
            jax.ShapeDtypeStruct((2 * QTR * TOK, lines), BF16),
        ),
        compiler_params=params(8),
        name="route",
    )(ids, w)


def dispatch_body(parts_ref, hid_ref, gain_ref, send_ref, res_ref, out_ref):
    total = parts_ref[0].astype(F32)
    for i in range(1, parts_ref.shape[0]):
        total = total + parts_ref[i].astype(F32)
    residual = hid_ref[...].reshape(TOK, D).astype(F32) + total
    res_ref[...] = residual
    mean = jnp.mean(residual * residual, axis=-1, keepdims=True)
    norm = (residual * lax.rsqrt(mean + 1e-06) * gain_ref[...].astype(F32)).astype(BF16)
    tall = jnp.concatenate([norm[:, q * WIDE : (q + 1) * WIDE] for q in range(QTR)], axis=0)
    out_ref[...] = dot(send_ref[...], tall).astype(BF16)


def dispatch(parts, hid, gain, send):
    return pl.pallas_call(
        dispatch_body,
        out_shape=(
            jax.ShapeDtypeStruct((TOK, D), F32),
            jax.ShapeDtypeStruct((send.shape[0], WIDE), BF16),
        ),
        compiler_params=params(14),
        name="dispatch",
    )(parts, hid, gain, send)


CHUNK = 512
PIECES = D // CHUNK


def expert_body(x, wg, wu, wd_hbm, out_ref, xs, wd, mid, res, sems):
    lines = x.shape[0]
    rows = lines // QTR
    group = rows // 4
    loads = []
    for c in range(PIECES):
        span = pl.ds(c * CHUNK, CHUNK)
        loads.append(pltpu.make_async_copy(wd_hbm.at[0, :, span], wd.at[:, span], sems.at[c]))
    for load in loads:
        load.start()
    n = lines // 4
    out_row, in_row = iota((n, n), 0), iota((n, n), 1)
    perm = (in_row == (out_row % group) * QTR + out_row // group).astype(BF16)
    unperm = (out_row == (in_row % group) * QTR + in_row // group).astype(BF16)
    for i in range(4):
        part = dot(perm, x[i * n : (i + 1) * n, :]).astype(BF16)
        for q in range(QTR):
            xs[i * group : (i + 1) * group, q * WIDE : (q + 1) * WIDE] = part[q * group : (q + 1) * group]
    gate = dot(xs[...], wg[0])
    gate = gate / (1.0 + jnp.exp(-gate))
    up = dot(xs[...], wu[0])
    mid[...] = (gate * up).astype(BF16)
    for c in range(PIECES):
        loads[c].wait()
        span = slice(c * CHUNK, (c + 1) * CHUNK)
        res[:, span] = dot(mid[...], wd[:, span]).astype(BF16)
    for i in range(4):
        part = [res[i * group : (i + 1) * group, q * WIDE : (q + 1) * WIDE] for q in range(QTR)]
        out_ref[i * n : (i + 1) * n, :] = dot(unperm, jnp.concatenate(part, axis=0)).astype(BF16)


def expert(x, wg, wu, wd):
    lines = x.shape[0]
    rows = lines // QTR
    vmem = pl.BlockSpec(memory_space=pltpu.VMEM)
    hbm = pl.BlockSpec(memory_space=pl.ANY)
    return pl.pallas_call(
        expert_body,
        in_specs=[vmem, vmem, vmem, hbm],
        out_specs=vmem,
        out_shape=jax.ShapeDtypeStruct(x.shape, BF16),
        scratch_shapes=[
            pltpu.VMEM((rows, D), BF16),
            pltpu.VMEM((FF, D), BF16),
            pltpu.VMEM((rows, FF), BF16),
            pltpu.VMEM((rows, D), BF16),
            pltpu.SemaphoreType.DMA((PIECES,)),
        ],
        compiler_params=params(36),
        cost_estimate=pl.CostEstimate(
            flops=6 * rows * D * FF, bytes_accessed=26 * 1024 * 1024, transcendentals=rows * FF
        ),
        name="expert",
    )(x, wg, wu, wd)


def combine_body(mix_ref, back_ref, res_ref, out_ref):
    both = dot(mix_ref[...], back_ref[...])
    n = QTR * TOK
    y = both[:n] + both[n:]
    for q in range(QTR):
        span = slice(q * WIDE, (q + 1) * WIDE)
        z = (res_ref[:, span] + y[q * TOK : (q + 1) * TOK]).astype(BF16)
        for s in range(TOK // STEPS):
            out_ref[0, s, :, span] = z[s * STEPS : (s + 1) * STEPS]


def combine(mix, back, res):
    return pl.pallas_call(
        combine_body,
        out_shape=jax.ShapeDtypeStruct((1, TOK // STEPS, STEPS, D), BF16),
        compiler_params=params(10),
        name="combine",
    )(mix, back, res)


def on_device(
    hidden,
    query,
    prefill_cache,
    suffix_cache,
    suffix_len,
    new_latent,
    w_uv,
    w_out,
    ffn_gain,
    expert_ids,
    route_weights,
    w_gate,
    w_up,
    w_down,
):
    samples = query.shape[1]
    n_smp = lax.axis_size("smp")
    chips = n_smp // 2
    prompts, _, width = prefill_cache.shape[1:]
    core = lax.axis_index("smp") % 2
    pair = [(i, i ^ 1) for i in range(n_smp)]
    same_core = [[2 * k + c for k in range(chips)] for c in range(2)]

    shared = n_smp // prompts // 2
    outgoing = pack(prefill_cache[0], shared).reshape(n_smp, LINES, 128)
    half_a = lax.all_to_all(outgoing, "smp", 0, 0, tiled=True)

    half_a, ids, weights, gain = lax.optimization_barrier((half_a, expert_ids, route_weights, ffn_gain))
    half_b = lax.ppermute(half_a, "smp", pair)
    send, mix = route(ids.reshape(TOK, TOP), weights.reshape(TOK, TOP))
    gain = gain.reshape(1, D)
    core = core.reshape(1)
    own = jnp.swapaxes(suffix_cache[0], 1, 2)
    q = query.reshape(samples, STEPS * HEADS, width)
    scored = score(suffix_len, q, half_a, own, new_latent[0])
    half_b, scored, send, mix, gain, core, w_uv, w_out = lax.optimization_barrier(
        (half_b, scored, send, mix, gain, core, w_uv, w_out)
    )
    uv_b = lax.ppermute(w_uv, "smp", pair)
    out_b = lax.ppermute(w_out, "smp", pair)
    context = attend(q, own, scored, half_a, half_b, new_latent[0])
    context, uv_b, out_b = lax.optimization_barrier((context, uv_b, out_b))
    by_chip = context.reshape(chips, HEADS // chips, TOK, LAT)
    by_heads = lax.all_to_all(by_chip, "smp", 0, 0, tiled=True, axis_index_groups=same_core)
    shares = project(core, by_heads, w_uv, uv_b, w_out, out_b)
    parts = lax.all_to_all(shares, "smp", 0, 0, tiled=True, axis_index_groups=same_core)
    residual, rows = dispatch(parts, hidden[0], gain, send)

    rows = rows.reshape(EXPERTS, 2 * QTR, WIDE)
    arrived = lax.all_to_all(rows, ("grp", "smp"), 0, 0, tiled=True)
    answered = expert(arrived.reshape(-1, WIDE), w_gate, w_up, w_down)
    answered = answered.reshape(EXPERTS, 2 * QTR, WIDE)
    returned = lax.all_to_all(answered, ("grp", "smp"), 0, 0, tiled=True)
    return combine(mix, returned.reshape(-1, WIDE), residual)


def solution(mesh):
    placed = (
        P("grp", "smp", None, None),
        P("grp", "smp", None, None, None),
        P("grp", None, "smp", None),
        P("grp", "smp", None, None),
        P("grp", "smp"),
        P("grp", "smp", None, None),
        P("smp", None, None),
        P("smp", None, None),
        P(),
        P("grp", "smp", None, None),
        P("grp", "smp", None, None),
        P(("grp", "smp"), None, None),
        P(("grp", "smp"), None, None),
        P(("grp", "smp"), None, None),
    )
    return jax.shard_map(
        on_device,
        mesh=mesh,
        in_specs=placed,
        out_specs=P("grp", "smp", None, None),
        check_vma=False,
    )
```

```python
import jax
import jax.numpy as jnp
from jax import lax
from jax.experimental import pallas as pl
from jax.experimental.pallas import tpu as pltpu
from jax.sharding import PartitionSpec as P

D = 3584
HEADS = 64
LAT = 512
ROPE = 64
NOPE = 128
FF = 1024
TOP = 8
STEPS = 4
SUF = 128
TOK = 16
EXPERTS = 128
QTR = 4
WIDE = D // QTR
SCALE = (NOPE + ROPE) ** (-0.5)
F32 = jnp.float32
BF16 = jnp.bfloat16
MIB = 1024 * 1024


def dot(a, b):
    return jnp.dot(a, b, preferred_element_type=F32)


def dot_t(a, b):
    return lax.dot_general(a, b, (((1,), (1,)), ((), ())), preferred_element_type=F32)


def iota(shape, dim):
    return lax.broadcasted_iota(jnp.int32, shape, dim)


def params(mib):
    return pltpu.CompilerParams(vmem_limit_bytes=mib * MIB)


SPAN = 32
LINES = SPAN * 4 + SPAN // 2
HALF = SPAN // 2


def pack_body(slab_ref, out_ref):
    prompts, span, _ = slab_ref.shape
    for p in range(prompts):
        for c in range(span // SPAN):
            x = slab_ref[p, c * SPAN : (c + 1) * SPAN, :]
            tiles = [x[:, i * 128 : (i + 1) * 128] for i in range(LAT // 128)]
            tiles.append(jnp.concatenate([x[:HALF, LAT:], x[HALF:, LAT:]], axis=1))
            block = jnp.concatenate(tiles, axis=0)
            for j in range(out_ref.shape[1]):
                out_ref[p, j, c] = block


def pack(slab, shared):
    prompts, span, _ = slab.shape
    vmem = pl.BlockSpec(memory_space=pltpu.VMEM)
    return pl.pallas_call(
        pack_body,
        in_specs=[vmem],
        out_specs=vmem,
        out_shape=jax.ShapeDtypeStruct((prompts, shared, span // SPAN, LINES, 128), BF16),
        compiler_params=params(8),
        name="pack",
    )(slab)


def latents(ref, g):
    tiles = [ref[:, i * SPAN + g * HALF : i * SPAN + (g + 1) * HALF, :] for i in range(LAT // 128)]
    return jnp.concatenate([t.reshape(-1, 128) for t in tiles], axis=1)


def keys(ref, g):
    return jnp.concatenate([latents(ref, g), ref[:, 4 * SPAN :, :].reshape(-1, 128)], axis=1)


def packed_scores(q, ref):
    gap = jnp.zeros((q.shape[0], ROPE), BF16)
    first = jnp.concatenate([q, gap], axis=1)
    second = jnp.concatenate([q[:, :LAT], gap, q[:, LAT:]], axis=1)
    return jnp.concatenate([dot_t(first, keys(ref, 0)), dot_t(second, keys(ref, 1))], axis=1)


def values(ref):
    return jnp.concatenate([latents(ref, 0), latents(ref, 1)], axis=0)


def score_body(len_ref, q_ref, ka_ref, own_ref, fresh_ref, sa_ref, so_ref, tail_ref):
    samples, rows, width = q_ref.shape
    col = iota((rows, 2 * SUF), 1)
    new = jnp.logical_and(col >= SUF, col - SUF <= iota((rows, 2 * SUF), 0) // HEADS)
    for s in range(samples):
        q = q_ref[s]
        sa_ref[s] = packed_scores(q, ka_ref)
        fresh = jnp.concatenate([fresh_ref[s].astype(F32), jnp.zeros((SUF - STEPS, width), F32)], axis=0)
        tail_ref[s, :, :SUF] = own_ref[s]
        tail_ref[s, :, SUF:] = fresh.T.astype(BF16)
        valid = jnp.logical_or(col < len_ref[0, s], new)
        so_ref[s] = jnp.where(valid, dot(q, tail_ref[s]), -jnp.inf)


def score(lens, q, ka, own, fresh):
    samples, rows, width = q.shape
    half = ka.shape[0] * SPAN
    vmem = pl.BlockSpec(memory_space=pltpu.VMEM)
    return pl.pallas_call(
        score_body,
        in_specs=[pl.BlockSpec(memory_space=pltpu.SMEM)] + [vmem] * 4,
        out_specs=[vmem] * 3,
        out_shape=(
            jax.ShapeDtypeStruct((samples, rows, half), F32),
            jax.ShapeDtypeStruct((samples, rows, 2 * SUF), F32),
            jax.ShapeDtypeStruct((samples, width, 2 * SUF), BF16),
        ),
        compiler_params=params(18),
        cost_estimate=pl.CostEstimate(
            flops=2 * samples * rows * (half + SUF) * width, bytes_accessed=2 * 1024 * 1024, transcendentals=0
        ),
        name="score",
    )(lens, q, ka, own, fresh)


def attend_body(q_ref, sa_ref, so_ref, tail_ref, ka_ref, kb_ref, out_ref, held):
    samples, rows, _ = q_ref.shape

    def settle(s, ahead):
        scores = [sa_ref[s], ahead, so_ref[s]]
        top = jnp.max(scores[0], -1, keepdims=True)
        for sc in scores[1:]:
            top = jnp.maximum(top, jnp.max(sc, -1, keepdims=True))
        total = jnp.zeros((rows, 1), F32)
        acc = jnp.zeros((rows, LAT), F32)
        for i, sc in enumerate(scores):
            p = jnp.exp((sc - top) * SCALE)
            total = total + jnp.sum(p, -1, keepdims=True)
            p = p.astype(BF16)
            if i == 2:
                acc = acc + dot_t(p, tail_ref[s, :LAT, :])
            else:
                acc = acc + dot(p, values((ka_ref, kb_ref)[i]))
        ctx = (acc / total).astype(BF16)
        for t in range(STEPS):
            held[s * STEPS + t] = ctx[t * HEADS : (t + 1) * HEADS]

    ahead = packed_scores(q_ref[0], kb_ref)
    for s in range(samples):
        now = ahead
        if s + 1 < samples:
            ahead = packed_scores(q_ref[s + 1], kb_ref)
        settle(s, now)
    n = TOK * 16
    perm = (iota((n, n), 1) == (iota((n, n), 0) % TOK) * 16 + iota((n, n), 0) // TOK).astype(BF16)
    for b in range(HEADS // 16):
        part = held[:, b * 16 : (b + 1) * 16, :].reshape(n, LAT)
        out_ref[b * 16 : (b + 1) * 16] = dot(perm, part).astype(BF16).reshape(16, TOK, LAT)


def attend(q, scored, ka, kb):
    samples, rows, width = q.shape
    half = ka.shape[0] * SPAN
    vmem = pl.BlockSpec(memory_space=pltpu.VMEM)
    return pl.pallas_call(
        attend_body,
        in_specs=[vmem] * 6,
        out_specs=vmem,
        out_shape=jax.ShapeDtypeStruct((HEADS, TOK, LAT), BF16),
        scratch_shapes=[pltpu.VMEM((TOK, HEADS, LAT), BF16)],
        compiler_params=params(30),
        cost_estimate=pl.CostEstimate(
            flops=2 * samples * rows * (half * width + (2 * half + SUF) * LAT),
            bytes_accessed=8 * 1024 * 1024,
            transcendentals=samples * rows * (2 * half + SUF),
        ),
        name="attend",
    )(q, *scored, ka, kb)


def project_body(core_ref, x_ref, uva_ref, uvb_ref, oa_ref, ob_ref, out_ref):
    chips, _, tok, _ = x_ref.shape
    rows = chips * tok
    core = core_ref[0]
    sides = []
    for side, uv in enumerate((uva_ref, uvb_ref)):
        first = 2 * core if side == 0 else 2 * (1 - core)
        cols = [dot(x_ref[:, pl.ds(first + h, 1)].reshape(rows, LAT), uv[h]).astype(BF16) for h in range(2)]
        sides.append(jnp.concatenate(cols, axis=1))
    both = jnp.concatenate(sides, axis=1)
    for c in range(D // 512):
        span = slice(c * 512, (c + 1) * 512)
        w = jnp.concatenate([o[:, :, span].reshape(2 * NOPE, 512) for o in (oa_ref, ob_ref)], axis=0)
        out_ref[:, :, span] = dot(both, w).astype(BF16).reshape(chips, tok, 512)


def project(core, x, uva, uvb, oa, ob):
    chips, _, tok, _ = x.shape
    vmem = pl.BlockSpec(memory_space=pltpu.VMEM)
    return pl.pallas_call(
        project_body,
        in_specs=[pl.BlockSpec(memory_space=pltpu.SMEM)] + [vmem] * 5,
        out_specs=vmem,
        out_shape=jax.ShapeDtypeStruct((chips, tok, D), BF16),
        compiler_params=params(20),
        cost_estimate=pl.CostEstimate(flops=1100000000, bytes_accessed=7 * 1024 * 1024, transcendentals=0),
        name="project",
    )(core, x, uva, uvb, oa, ob)


def route_body(ids_ref, w_ref, send_ref, mix_ref):
    lines = EXPERTS * 2 * QTR
    ids = ids_ref[...]
    w = w_ref[...]
    lane = iota((TOK, EXPERTS), 1)
    named = jnp.zeros((TOK, EXPERTS), F32)
    weight = jnp.zeros((TOK, EXPERTS), F32)
    for k in range(TOP):
        hit = ids[:, k : k + 1] == lane
        named = named + jnp.where(hit, 1.0, 0.0)
        weight = weight + jnp.where(hit, w[:, k : k + 1], 0.0)
    below = (iota((TOK, TOK), 1) < iota((TOK, TOK), 0)).astype(BF16)
    earlier = dot(below, named.astype(BF16))
    spread = (iota((EXPERTS, lines), 1) // (2 * QTR) == iota((EXPERTS, lines), 0)).astype(BF16)
    high = weight.astype(BF16)
    low = (weight - high.astype(F32)).astype(BF16)
    stack = jnp.concatenate([named.astype(BF16), earlier.astype(BF16), high, low], axis=0)
    wide = dot(stack, spread)
    named, earlier, high, low = (wide[i * TOK : (i + 1) * TOK] for i in range(4))
    col = iota((TOK, lines), 1)
    slot = (col % (2 * QTR)) // QTR
    chosen = jnp.logical_and(named > 0.5, jnp.abs(earlier - slot.astype(F32)) < 0.5)
    sel = []
    for q in range(QTR):
        here = jnp.logical_and(chosen, col % QTR == q)
        sel.append(jnp.where(here, 1.0, 0.0))
        mix_ref[q * TOK : (q + 1) * TOK, :] = jnp.where(here, high, 0.0).astype(BF16)
        mix_ref[(QTR + q) * TOK : (QTR + q + 1) * TOK, :] = jnp.where(here, low, 0.0).astype(BF16)
    send_ref[...] = jnp.concatenate(sel, axis=0).T.astype(BF16)


def route(ids, w):
    lines = EXPERTS * 2 * QTR
    return pl.pallas_call(
        route_body,
        out_shape=(
            jax.ShapeDtypeStruct((lines, QTR * TOK), BF16),
            jax.ShapeDtypeStruct((2 * QTR * TOK, lines), BF16),
        ),
        compiler_params=params(8),
        name="route",
    )(ids, w)


def dispatch_body(parts_ref, hid_ref, gain_ref, send_ref, res_ref, out_ref):
    total = parts_ref[0].astype(F32)
    for i in range(1, parts_ref.shape[0]):
        total = total + parts_ref[i].astype(F32)
    residual = hid_ref[...].reshape(TOK, D).astype(F32) + total
    res_ref[...] = residual
    mean = jnp.mean(residual * residual, axis=-1, keepdims=True)
    norm = (residual * lax.rsqrt(mean + 1e-06) * gain_ref[...].astype(F32)).astype(BF16)
    tall = jnp.concatenate([norm[:, q * WIDE : (q + 1) * WIDE] for q in range(QTR)], axis=0)
    out_ref[...] = dot(send_ref[...], tall).astype(BF16)


def dispatch(parts, hid, gain, send):
    return pl.pallas_call(
        dispatch_body,
        out_shape=(
            jax.ShapeDtypeStruct((TOK, D), F32),
            jax.ShapeDtypeStruct((send.shape[0], WIDE), BF16),
        ),
        compiler_params=params(14),
        name="dispatch",
    )(parts, hid, gain, send)


CHUNK = 512
PIECES = D // CHUNK
LOADS = 4


def expert_body(x, wg, wu, wd_hbm, out_ref, xs, wd, mid, res, sems):
    lines = x.shape[0]
    rows = lines // QTR
    group = rows // 4
    loads = []
    for c in range(LOADS):
        span = pl.ds(c * (FF // LOADS), FF // LOADS)
        loads.append(pltpu.make_async_copy(wd_hbm.at[0, span, :], wd.at[span, :], sems.at[c]))
    for load in loads:
        load.start()
    n = lines // 4
    out_row, in_row = iota((n, n), 0), iota((n, n), 1)
    perm = (in_row == (out_row % group) * QTR + out_row // group).astype(BF16)
    unperm = (out_row == (in_row % group) * QTR + in_row // group).astype(BF16)
    for i in range(4):
        part = dot(perm, x[i * n : (i + 1) * n, :]).astype(BF16)
        for q in range(QTR):
            xs[i * group : (i + 1) * group, q * WIDE : (q + 1) * WIDE] = part[q * group : (q + 1) * group]
    for f in range(4):
        span = slice(f * 256, (f + 1) * 256)
        gate = dot(xs[...], wg[0, :, span])
        up = dot(xs[...], wu[0, :, span])
        mid[:, span] = (gate / (1.0 + jnp.exp(-gate)) * up).astype(BF16)
    for load in loads:
        load.wait()
    for c in range(PIECES):
        span = slice(c * CHUNK, (c + 1) * CHUNK)
        res[:, span] = dot(mid[...], wd[:, span]).astype(BF16)
    for i in range(4):
        part = [res[i * group : (i + 1) * group, q * WIDE : (q + 1) * WIDE] for q in range(QTR)]
        out_ref[i * n : (i + 1) * n, :] = dot(unperm, jnp.concatenate(part, axis=0)).astype(BF16)


def expert(x, wg, wu, wd):
    lines = x.shape[0]
    rows = lines // QTR
    vmem = pl.BlockSpec(memory_space=pltpu.VMEM)
    hbm = pl.BlockSpec(memory_space=pl.ANY)
    return pl.pallas_call(
        expert_body,
        in_specs=[vmem, vmem, vmem, hbm],
        out_specs=vmem,
        out_shape=jax.ShapeDtypeStruct(x.shape, BF16),
        scratch_shapes=[
            pltpu.VMEM((rows, D), BF16),
            pltpu.VMEM((FF, D), BF16),
            pltpu.VMEM((rows, FF), BF16),
            pltpu.VMEM((rows, D), BF16),
            pltpu.SemaphoreType.DMA((LOADS,)),
        ],
        compiler_params=params(36),
        cost_estimate=pl.CostEstimate(
            flops=6 * rows * D * FF, bytes_accessed=26 * 1024 * 1024, transcendentals=rows * FF
        ),
        name="expert",
    )(x, wg, wu, wd)


def combine_body(mix_ref, back_ref, res_ref, out_ref):
    both = dot(mix_ref[...], back_ref[...])
    n = QTR * TOK
    y = both[:n] + both[n:]
    for q in range(QTR):
        span = slice(q * WIDE, (q + 1) * WIDE)
        z = (res_ref[:, span] + y[q * TOK : (q + 1) * TOK]).astype(BF16)
        for s in range(TOK // STEPS):
            out_ref[0, s, :, span] = z[s * STEPS : (s + 1) * STEPS]


def combine(mix, back, res):
    return pl.pallas_call(
        combine_body,
        out_shape=jax.ShapeDtypeStruct((1, TOK // STEPS, STEPS, D), BF16),
        compiler_params=params(10),
        name="combine",
    )(mix, back, res)


def on_device(
    hidden,
    query,
    prefill_cache,
    suffix_cache,
    suffix_len,
    new_latent,
    w_uv,
    w_out,
    ffn_gain,
    expert_ids,
    route_weights,
    w_gate,
    w_up,
    w_down,
):
    samples = query.shape[1]
    n_smp = lax.axis_size("smp")
    chips = n_smp // 2
    prompts, _, width = prefill_cache.shape[1:]
    core = lax.axis_index("smp") % 2
    pair = [(i, i ^ 1) for i in range(n_smp)]
    same_core = [[2 * k + c for k in range(chips)] for c in range(2)]

    shared = n_smp // prompts // 2
    outgoing = pack(prefill_cache[0], shared).reshape(n_smp, LINES, 128)
    half_a = lax.all_to_all(outgoing, "smp", 0, 0, tiled=True)

    half_a, ids, weights, gain = lax.optimization_barrier((half_a, expert_ids, route_weights, ffn_gain))
    half_b = lax.ppermute(half_a, "smp", pair)
    send, mix = route(ids.reshape(TOK, TOP), weights.reshape(TOK, TOP))
    gain = gain.reshape(1, D)
    core = core.reshape(1)
    own = jnp.swapaxes(suffix_cache[0], 1, 2)
    q = query.reshape(samples, STEPS * HEADS, width)
    scored = score(suffix_len, q, half_a, own, new_latent[0])
    half_b, scored, send, mix, gain, core, w_uv, w_out = lax.optimization_barrier(
        (half_b, scored, send, mix, gain, core, w_uv, w_out)
    )
    uv_b = lax.ppermute(w_uv, "smp", pair)
    out_b = lax.ppermute(w_out, "smp", pair)
    context = attend(q, scored, half_a, half_b)
    context, uv_b, out_b = lax.optimization_barrier((context, uv_b, out_b))
    by_chip = context.reshape(chips, HEADS // chips, TOK, LAT)
    by_heads = lax.all_to_all(by_chip, "smp", 0, 0, tiled=True, axis_index_groups=same_core)
    shares = project(core, by_heads, w_uv, uv_b, w_out, out_b)
    parts = lax.all_to_all(shares, "smp", 0, 0, tiled=True, axis_index_groups=same_core)
    residual, rows = dispatch(parts, hidden[0], gain, send)

    rows = rows.reshape(EXPERTS, 2 * QTR, WIDE)
    arrived = lax.all_to_all(rows, ("grp", "smp"), 0, 0, tiled=True)
    answered = expert(arrived.reshape(-1, WIDE), w_gate, w_up, w_down)
    answered = answered.reshape(EXPERTS, 2 * QTR, WIDE)
    returned = lax.all_to_all(answered, ("grp", "smp"), 0, 0, tiled=True)
    return combine(mix, returned.reshape(-1, WIDE), residual)


def solution(mesh):
    placed = (
        P("grp", "smp", None, None),
        P("grp", "smp", None, None, None),
        P("grp", None, "smp", None),
        P("grp", "smp", None, None),
        P("grp", "smp"),
        P("grp", "smp", None, None),
        P("smp", None, None),
        P("smp", None, None),
        P(),
        P("grp", "smp", None, None),
        P("grp", "smp", None, None),
        P(("grp", "smp"), None, None),
        P(("grp", "smp"), None, None),
        P(("grp", "smp"), None, None),
    )
    return jax.shard_map(
        on_device,
        mesh=mesh,
        in_specs=placed,
        out_specs=P("grp", "smp", None, None),
        check_vma=False,
    )
```

```python
import jax
import jax.numpy as jnp
from jax import lax
from jax.experimental import pallas as pl
from jax.experimental.pallas import tpu as pltpu
from jax.sharding import PartitionSpec as P

D = 3584
HEADS = 64
LAT = 512
ROPE = 64
NOPE = 128
FF = 1024
TOP = 8
STEPS = 4
SUF = 128
TOK = 16
EXPERTS = 128
QTR = 4
WIDE = D // QTR
SCALE = (NOPE + ROPE) ** (-0.5)
F32 = jnp.float32
BF16 = jnp.bfloat16
MIB = 1024 * 1024


def dot(a, b):
    return jnp.dot(a, b, preferred_element_type=F32)


def dot_t(a, b):
    return lax.dot_general(a, b, (((1,), (1,)), ((), ())), preferred_element_type=F32)


def iota(shape, dim):
    return lax.broadcasted_iota(jnp.int32, shape, dim)


def params(mib):
    return pltpu.CompilerParams(vmem_limit_bytes=mib * MIB)


SPAN = 32
LINES = SPAN * 4 + SPAN // 2
HALF = SPAN // 2


def pack_body(slab_ref, out_ref):
    prompts, span, _ = slab_ref.shape
    for p in range(prompts):
        for c in range(span // SPAN):
            x = slab_ref[p, c * SPAN : (c + 1) * SPAN, :]
            tiles = [x[:, i * 128 : (i + 1) * 128] for i in range(LAT // 128)]
            tiles.append(jnp.concatenate([x[:HALF, LAT:], x[HALF:, LAT:]], axis=1))
            block = jnp.concatenate(tiles, axis=0)
            for j in range(out_ref.shape[1]):
                out_ref[p, j, c] = block


def pack(slab, shared):
    prompts, span, _ = slab.shape
    vmem = pl.BlockSpec(memory_space=pltpu.VMEM)
    return pl.pallas_call(
        pack_body,
        in_specs=[vmem],
        out_specs=vmem,
        out_shape=jax.ShapeDtypeStruct((prompts, shared, span // SPAN, LINES, 128), BF16),
        compiler_params=params(8),
        name="pack",
    )(slab)


def latents(ref, g):
    tiles = [ref[:, i * SPAN + g * HALF : i * SPAN + (g + 1) * HALF, :] for i in range(LAT // 128)]
    return jnp.concatenate([t.reshape(-1, 128) for t in tiles], axis=1)


def keys(ref, g):
    return jnp.concatenate([latents(ref, g), ref[:, 4 * SPAN :, :].reshape(-1, 128)], axis=1)


def packed_scores(q, ref):
    gap = jnp.zeros((q.shape[0], ROPE), BF16)
    first = jnp.concatenate([q, gap], axis=1)
    second = jnp.concatenate([q[:, :LAT], gap, q[:, LAT:]], axis=1)
    return jnp.concatenate([dot_t(first, keys(ref, 0)), dot_t(second, keys(ref, 1))], axis=1)


def values(ref):
    return jnp.concatenate([latents(ref, 0), latents(ref, 1)], axis=0)


def score_body(len_ref, q_ref, ka_ref, own_ref, fresh_ref, sa_ref, so_ref, tail_ref):
    samples, rows, width = q_ref.shape
    col = iota((rows, 2 * SUF), 1)
    new = jnp.logical_and(col >= SUF, col - SUF <= iota((rows, 2 * SUF), 0) // HEADS)
    for s in range(samples):
        q = q_ref[s]
        sa_ref[s] = packed_scores(q, ka_ref)
        fresh = jnp.concatenate([fresh_ref[s].astype(F32), jnp.zeros((SUF - STEPS, width), F32)], axis=0)
        tail_ref[s, :, :SUF] = own_ref[s]
        tail_ref[s, :, SUF:] = fresh.T.astype(BF16)
        valid = jnp.logical_or(col < len_ref[0, s], new)
        so_ref[s] = jnp.where(valid, dot(q, tail_ref[s]), -jnp.inf)


def score(lens, q, ka, own, fresh):
    samples, rows, width = q.shape
    half = ka.shape[0] * SPAN
    vmem = pl.BlockSpec(memory_space=pltpu.VMEM)
    return pl.pallas_call(
        score_body,
        in_specs=[pl.BlockSpec(memory_space=pltpu.SMEM)] + [vmem] * 4,
        out_specs=[vmem] * 3,
        out_shape=(
            jax.ShapeDtypeStruct((samples, rows, half), F32),
            jax.ShapeDtypeStruct((samples, rows, 2 * SUF), F32),
            jax.ShapeDtypeStruct((samples, width, 2 * SUF), BF16),
        ),
        compiler_params=params(18),
        cost_estimate=pl.CostEstimate(
            flops=2 * samples * rows * (half + SUF) * width, bytes_accessed=2 * 1024 * 1024, transcendentals=0
        ),
        name="score",
    )(lens, q, ka, own, fresh)


def attend_body(q_ref, sa_ref, so_ref, tail_ref, ka_ref, kb_ref, out_ref, held):
    samples, rows, _ = q_ref.shape

    def settle(s, ahead):
        scores = [sa_ref[s], ahead, so_ref[s]]
        top = jnp.max(scores[0], -1, keepdims=True)
        for sc in scores[1:]:
            top = jnp.maximum(top, jnp.max(sc, -1, keepdims=True))
        total = jnp.zeros((rows, 1), F32)
        acc = jnp.zeros((rows, LAT), F32)
        for i, sc in enumerate(scores):
            p = jnp.exp((sc - top) * SCALE)
            total = total + jnp.sum(p, -1, keepdims=True)
            p = p.astype(BF16)
            if i == 2:
                acc = acc + dot_t(p, tail_ref[s, :LAT, :])
            else:
                acc = acc + dot(p, values((ka_ref, kb_ref)[i]))
        ctx = (acc / total).astype(BF16)
        for t in range(STEPS):
            held[s * STEPS + t] = ctx[t * HEADS : (t + 1) * HEADS]

    ahead = packed_scores(q_ref[0], kb_ref)
    for s in range(samples):
        now = ahead
        if s + 1 < samples:
            ahead = packed_scores(q_ref[s + 1], kb_ref)
        settle(s, now)
    n = TOK * 16
    perm = (iota((n, n), 1) == (iota((n, n), 0) % TOK) * 16 + iota((n, n), 0) // TOK).astype(BF16)
    for b in range(HEADS // 16):
        part = held[:, b * 16 : (b + 1) * 16, :].reshape(n, LAT)
        out_ref[b * 16 : (b + 1) * 16] = dot(perm, part).astype(BF16).reshape(16, TOK, LAT)


def attend(q, scored, ka, kb):
    samples, rows, width = q.shape
    half = ka.shape[0] * SPAN
    vmem = pl.BlockSpec(memory_space=pltpu.VMEM)
    return pl.pallas_call(
        attend_body,
        in_specs=[vmem] * 6,
        out_specs=vmem,
        out_shape=jax.ShapeDtypeStruct((HEADS, TOK, LAT), BF16),
        scratch_shapes=[pltpu.VMEM((TOK, HEADS, LAT), BF16)],
        compiler_params=params(30),
        cost_estimate=pl.CostEstimate(
            flops=2 * samples * rows * (half * width + (2 * half + SUF) * LAT),
            bytes_accessed=8 * 1024 * 1024,
            transcendentals=samples * rows * (2 * half + SUF),
        ),
        name="attend",
    )(q, *scored, ka, kb)


def project_body(core_ref, x_ref, uva_ref, uvb_ref, oa_ref, ob_ref, out_ref):
    chips, _, tok, _ = x_ref.shape
    rows = chips * tok
    core = core_ref[0]
    sides = []
    for side, uv in enumerate((uva_ref, uvb_ref)):
        first = 2 * core if side == 0 else 2 * (1 - core)
        cols = [dot(x_ref[:, pl.ds(first + h, 1)].reshape(rows, LAT), uv[h]).astype(BF16) for h in range(2)]
        sides.append(jnp.concatenate(cols, axis=1))
    both = jnp.concatenate(sides, axis=1)
    for c in range(D // 512):
        span = slice(c * 512, (c + 1) * 512)
        w = jnp.concatenate([o[:, :, span].reshape(2 * NOPE, 512) for o in (oa_ref, ob_ref)], axis=0)
        out_ref[:, :, span] = dot(both, w).astype(BF16).reshape(chips, tok, 512)


def project(core, x, uva, uvb, oa, ob):
    chips, _, tok, _ = x.shape
    vmem = pl.BlockSpec(memory_space=pltpu.VMEM)
    return pl.pallas_call(
        project_body,
        in_specs=[pl.BlockSpec(memory_space=pltpu.SMEM)] + [vmem] * 5,
        out_specs=vmem,
        out_shape=jax.ShapeDtypeStruct((chips, tok, D), BF16),
        compiler_params=params(20),
        cost_estimate=pl.CostEstimate(flops=1100000000, bytes_accessed=7 * 1024 * 1024, transcendentals=0),
        name="project",
    )(core, x, uva, uvb, oa, ob)


def route_body(ids_ref, w_ref, send_ref, mix_ref):
    lines = EXPERTS * 2 * QTR
    ids = ids_ref[...]
    w = w_ref[...]
    lane = iota((TOK, EXPERTS), 1)
    named = jnp.zeros((TOK, EXPERTS), F32)
    weight = jnp.zeros((TOK, EXPERTS), F32)
    for k in range(TOP):
        hit = ids[:, k : k + 1] == lane
        named = named + jnp.where(hit, 1.0, 0.0)
        weight = weight + jnp.where(hit, w[:, k : k + 1], 0.0)
    below = (iota((TOK, TOK), 1) < iota((TOK, TOK), 0)).astype(BF16)
    earlier = dot(below, named.astype(BF16))
    spread = (iota((EXPERTS, lines), 1) // (2 * QTR) == iota((EXPERTS, lines), 0)).astype(BF16)
    high = weight.astype(BF16)
    low = (weight - high.astype(F32)).astype(BF16)
    stack = jnp.concatenate([named.astype(BF16), earlier.astype(BF16), high, low], axis=0)
    wide = dot(stack, spread)
    named, earlier, high, low = (wide[i * TOK : (i + 1) * TOK] for i in range(4))
    col = iota((TOK, lines), 1)
    slot = (col % (2 * QTR)) // QTR
    chosen = jnp.logical_and(named > 0.5, jnp.abs(earlier - slot.astype(F32)) < 0.5)
    sel = []
    for q in range(QTR):
        here = jnp.logical_and(chosen, col % QTR == q)
        sel.append(jnp.where(here, 1.0, 0.0))
        mix_ref[q * TOK : (q + 1) * TOK, :] = jnp.where(here, high, 0.0).astype(BF16)
        mix_ref[(QTR + q) * TOK : (QTR + q + 1) * TOK, :] = jnp.where(here, low, 0.0).astype(BF16)
    send_ref[...] = jnp.concatenate(sel, axis=0).T.astype(BF16)


def route(ids, w):
    lines = EXPERTS * 2 * QTR
    return pl.pallas_call(
        route_body,
        out_shape=(
            jax.ShapeDtypeStruct((lines, QTR * TOK), BF16),
            jax.ShapeDtypeStruct((2 * QTR * TOK, lines), BF16),
        ),
        compiler_params=params(8),
        name="route",
    )(ids, w)


def dispatch_body(parts_ref, hid_ref, gain_ref, send_ref, res_ref, out_ref):
    total = parts_ref[0].astype(F32)
    for i in range(1, parts_ref.shape[0]):
        total = total + parts_ref[i].astype(F32)
    residual = hid_ref[...].reshape(TOK, D).astype(F32) + total
    res_ref[...] = residual
    mean = jnp.mean(residual * residual, axis=-1, keepdims=True)
    norm = (residual * lax.rsqrt(mean + 1e-06) * gain_ref[...].astype(F32)).astype(BF16)
    tall = jnp.concatenate([norm[:, q * WIDE : (q + 1) * WIDE] for q in range(QTR)], axis=0)
    out_ref[...] = dot(send_ref[...], tall).astype(BF16)


def dispatch(parts, hid, gain, send):
    return pl.pallas_call(
        dispatch_body,
        out_shape=(
            jax.ShapeDtypeStruct((TOK, D), F32),
            jax.ShapeDtypeStruct((send.shape[0], WIDE), BF16),
        ),
        compiler_params=params(14),
        name="dispatch",
    )(parts, hid, gain, send)


CHUNK = 512
PIECES = D // CHUNK


def expert_body(x, wg, wu, wd, out_ref, xs, mid, res):
    lines = x.shape[0]
    rows = lines // QTR
    group = rows // 4
    n = lines // 4
    out_row, in_row = iota((n, n), 0), iota((n, n), 1)
    perm = (in_row == (out_row % group) * QTR + out_row // group).astype(BF16)
    unperm = (out_row == (in_row % group) * QTR + in_row // group).astype(BF16)
    for i in range(4):
        part = dot(perm, x[i * n : (i + 1) * n, :]).astype(BF16)
        for q in range(QTR):
            xs[i * group : (i + 1) * group, q * WIDE : (q + 1) * WIDE] = part[q * group : (q + 1) * group]
    for f in range(2):
        span = slice(f * 512, (f + 1) * 512)
        gate = dot(xs[...], wg[0, :, span])
        up = dot(xs[...], wu[0, :, span])
        mid[:, span] = (gate / (1.0 + jnp.exp(-gate)) * up).astype(BF16)
    for c in range(PIECES):
        res[:, c * CHUNK : (c + 1) * CHUNK] = dot(mid[...], wd[0, :, c * CHUNK : (c + 1) * CHUNK]).astype(BF16)
    for i in range(4):
        part = [res[i * group : (i + 1) * group, q * WIDE : (q + 1) * WIDE] for q in range(QTR)]
        out_ref[i * n : (i + 1) * n, :] = dot(unperm, jnp.concatenate(part, axis=0)).astype(BF16)


def expert(x, wg, wu, wd):
    lines = x.shape[0]
    rows = lines // QTR
    vmem = pl.BlockSpec(memory_space=pltpu.VMEM)
    return pl.pallas_call(
        expert_body,
        in_specs=[vmem] * 4,
        out_specs=vmem,
        out_shape=jax.ShapeDtypeStruct(x.shape, BF16),
        scratch_shapes=[
            pltpu.VMEM((rows, D), BF16),
            pltpu.VMEM((rows, FF), BF16),
            pltpu.VMEM((rows, D), BF16),
        ],
        compiler_params=params(26),
        cost_estimate=pl.CostEstimate(
            flops=6 * rows * D * FF, bytes_accessed=26 * 1024 * 1024, transcendentals=rows * FF
        ),
        name="expert",
    )(x, wg, wu, wd)


def combine_body(mix_ref, back_ref, res_ref, out_ref):
    both = dot(mix_ref[...], back_ref[...])
    n = QTR * TOK
    y = both[:n] + both[n:]
    for q in range(QTR):
        span = slice(q * WIDE, (q + 1) * WIDE)
        z = (res_ref[:, span] + y[q * TOK : (q + 1) * TOK]).astype(BF16)
        for s in range(TOK // STEPS):
            out_ref[0, s, :, span] = z[s * STEPS : (s + 1) * STEPS]


def combine(mix, back, res):
    return pl.pallas_call(
        combine_body,
        out_shape=jax.ShapeDtypeStruct((1, TOK // STEPS, STEPS, D), BF16),
        compiler_params=params(10),
        name="combine",
    )(mix, back, res)


def on_device(
    hidden,
    query,
    prefill_cache,
    suffix_cache,
    suffix_len,
    new_latent,
    w_uv,
    w_out,
    ffn_gain,
    expert_ids,
    route_weights,
    w_gate,
    w_up,
    w_down,
):
    samples = query.shape[1]
    n_smp = lax.axis_size("smp")
    chips = n_smp // 2
    prompts, _, width = prefill_cache.shape[1:]
    core = lax.axis_index("smp") % 2
    pair = [(i, i ^ 1) for i in range(n_smp)]
    same_core = [[2 * k + c for k in range(chips)] for c in range(2)]

    shared = n_smp // prompts // 2
    outgoing = pack(prefill_cache[0], shared).reshape(n_smp, LINES, 128)
    half_a = lax.all_to_all(outgoing, "smp", 0, 0, tiled=True)

    half_a, ids, weights, gain = lax.optimization_barrier((half_a, expert_ids, route_weights, ffn_gain))
    half_b = lax.ppermute(half_a, "smp", pair)
    send, mix = route(ids.reshape(TOK, TOP), weights.reshape(TOK, TOP))
    gain = gain.reshape(1, D)
    core = core.reshape(1)
    own = jnp.swapaxes(suffix_cache[0], 1, 2)
    q = query.reshape(samples, STEPS * HEADS, width)
    scored = score(suffix_len, q, half_a, own, new_latent[0])
    half_b, scored, send, mix, gain, core, w_uv, w_out = lax.optimization_barrier(
        (half_b, scored, send, mix, gain, core, w_uv, w_out)
    )
    uv_b = lax.ppermute(w_uv, "smp", pair)
    out_b = lax.ppermute(w_out, "smp", pair)
    context = attend(q, scored, half_a, half_b)
    context, uv_b, out_b = lax.optimization_barrier((context, uv_b, out_b))
    by_chip = context.reshape(chips, HEADS // chips, TOK, LAT)
    by_heads = lax.all_to_all(by_chip, "smp", 0, 0, tiled=True, axis_index_groups=same_core)
    shares = project(core, by_heads, w_uv, uv_b, w_out, out_b)
    parts = lax.all_to_all(shares, "smp", 0, 0, tiled=True, axis_index_groups=same_core)
    residual, rows = dispatch(parts, hidden[0], gain, send)

    rows = rows.reshape(EXPERTS, 2 * QTR, WIDE)
    arrived = lax.all_to_all(rows, ("grp", "smp"), 0, 0, tiled=True)
    answered = expert(arrived.reshape(-1, WIDE), w_gate, w_up, w_down)
    answered = answered.reshape(EXPERTS, 2 * QTR, WIDE)
    returned = lax.all_to_all(answered, ("grp", "smp"), 0, 0, tiled=True)
    return combine(mix, returned.reshape(-1, WIDE), residual)


def solution(mesh):
    placed = (
        P("grp", "smp", None, None),
        P("grp", "smp", None, None, None),
        P("grp", None, "smp", None),
        P("grp", "smp", None, None),
        P("grp", "smp"),
        P("grp", "smp", None, None),
        P("smp", None, None),
        P("smp", None, None),
        P(),
        P("grp", "smp", None, None),
        P("grp", "smp", None, None),
        P(("grp", "smp"), None, None),
        P(("grp", "smp"), None, None),
        P(("grp", "smp"), None, None),
    )
    return jax.shard_map(
        on_device,
        mesh=mesh,
        in_specs=placed,
        out_specs=P("grp", "smp", None, None),
        check_vma=False,
    )
```
